128 devices in a mesh: outer: 16 (over z, y), inner: 4 (over x_lo, core), head: 2 (over x_hi).
Axes of the slice: x: 4 (x_hi: 2, x_lo: 2; x = x_hi * 2 + x_lo), y: 4, z: 4, core: 2. Of those that a mesh axis runs over, the one named last changes fastest.
Arguments:
- queries: bfloat16 [16384, 4096], P(('outer', 'inner'), 'head'), may hold values from -6 to 6
- key_heads: bfloat16 [16384, 1024], P(('outer', 'inner', 'head')), may hold values from -6 to 6
- value_heads: bfloat16 [16384, 1024], P(('outer', 'inner', 'head')), may hold values from -6 to 6
- output: bfloat16 [16384, 4096], P(('outer', 'inner'), 'head'), may hold values from -1.5 to 1.5
- output_grad: bfloat16 [16384, 4096], P(('outer', 'inner'), 'head'), may hold values from -192 to 192
- log_totals: float32 [32, 16384], P('head', ('outer', 'inner')), may hold values from 7 to 8.5
- random_blocks: int32 [128, 3], P(('outer', 'inner')), may hold values from 0 to 127, as said below
- window_width: int32 [128], P(('outer', 'inner')), may hold values from 1 to 2, as said below
- global_blocks: int32 [2], replicated, may hold values from 0 to 127
Outputs:
- query_grad: bfloat16 [16384, 4096], P(('outer', 'inner'), 'head')
- key_grad: bfloat16 [16384, 1024], P(('outer', 'inner', 'head'))
- value_grad: bfloat16 [16384, 1024], P(('outer', 'inner', 'head'))
The draws below stay inside these ranges and needn't reach their ends.
Inputs may be any that keep to these rules, and one draw needn't show every extreme that they name: `random_blocks`: number the sequence shards of 256 tokens s = 0, 1, ... The random key blocks of query blocks of shard s lie in shards s2 with s2 % 4 == s % 4; the 6 random entries of shard s name distinct key blocks, at most 2 of them in any one shard and exactly 2 in at least one. `window_width`: the value 2 occurs in every draw.
All inputs are finite; a program needn't handle non-finite values.
Results may differ from the reference program's by a relative error of at most 0.0053.
Values may be sent and summed in bfloat16 or wider, within the bound.
A program may use at most 128 MiB of HBM per device.

```python
import jax
import jax.numpy as jnp
from jax import lax

HEADS = 32
KV_HEADS = 8
HDIM = 128
BLOCK = 128
WIN = 2
GLOB = 2
RAND = 3
NB = 2
LIST = 10
SEQ = 16384
NBLK = 128
CAP = 2
N_OUTER = 16
N_INNER = 4


def draw_random_blocks(key, part):
    key = jax.random.fold_in(key, 11)
    slot_total = N_OUTER * CAP
    entry_total = NB * RAND

    def one_shard(shard_index):
        shard_key = jax.random.fold_in(key, shard_index)
        full_key, order_key, local_key, place_key = jax.random.split(shard_key, 4)
        full_owner = jax.random.randint(full_key, (), 0, N_OUTER)
        priority = jax.random.permutation(order_key, slot_total)
        slot_owner = jnp.arange(slot_total) // CAP
        ranked = jnp.where(slot_owner == full_owner, priority - slot_total, priority)
        chosen = jnp.argsort(ranked, stable=True)[:entry_total]
        local_orders = jax.vmap(lambda single: jax.random.permutation(single, NB))(jax.random.split(local_key, N_OUTER))
        chosen_owner = chosen // CAP
        chosen_local = local_orders[chosen_owner, chosen % CAP]
        shard_ids = (chosen_owner * N_INNER + shard_index % N_INNER) * NB + chosen_local
        placing = jax.random.permutation(place_key, entry_total)
        return shard_ids[placing].reshape(NB, RAND)
    blocks = jax.vmap(one_shard)(jnp.arange(N_OUTER * N_INNER))
    return blocks.reshape(NBLK, RAND).astype(jnp.int32)


def draw_window_width(key, part):
    key = jax.random.fold_in(key, 23)
    width_key, spot_key = jax.random.split(key)
    widths = jax.random.randint(width_key, (NBLK,), 1, WIN + 1)
    spot = jax.random.randint(spot_key, (), 0, NBLK)
    return widths.at[spot].set(WIN).astype(jnp.int32)


def levels(rng, shape, shards, smallest, high):
    def one(axis_at, parts):
        draws = jax.random.uniform(jax.random.fold_in(jax.random.fold_in(rng, 6), axis_at), (parts,), jnp.float32, smallest / len(shards), high / len(shards))
        return jnp.repeat(jnp.exp(draws), shape[axis_at] // parts).reshape((-1,) + (1,) * (len(shape) - axis_at - 1))

    factor_of = one(*shards[0])
    for cut in shards[1:]:
        factor_of = factor_of * one(*cut)
    return factor_of


def bell_draw(own_key, shape, scale, most, shards=(), held_as=jnp.bfloat16):
    drawn = jax.random.normal(own_key, shape, jnp.float32) * scale
    if len(shards) > 0:
        drawn = levels(own_key, shape, shards, -0.22, 0.18) * drawn
    return jnp.clip(drawn, min=-most, max=most).astype(held_as)


def setup_inputs(seed: int = 0) -> dict:
    keys = jax.random.split(jax.random.key(seed), 10)
    queries = bell_draw(keys[0], (SEQ, HEADS * HDIM), 1.0, 6.0, ((0, 64), (1, 2)))
    key_heads = bell_draw(keys[1], (SEQ, KV_HEADS * HDIM), 1.0, 6.0, ((0, 128),))
    value_heads = bell_draw(keys[2], (SEQ, KV_HEADS * HDIM), 1.0, 6.0, ((0, 128),))
    output = bell_draw(keys[3], (SEQ, HEADS * HDIM), 0.1, 1.5, ((0, 64), (1, 2)))
    output_grad = bell_draw(keys[4], (SEQ, HEADS * HDIM), 32.0, 192.0, ((0, 64), (1, 2)))
    log_totals = jnp.clip(7.0 + 1.5 * jax.random.uniform(keys[5], (HEADS, SEQ), jnp.float32) ** levels(keys[5], (HEADS, SEQ), ((0, 2), (1, 64)), -0.2, 0.2), 7.0, 8.5)
    random_blocks = draw_random_blocks(jax.random.fold_in(keys[9], 71), 0)
    window_width = draw_window_width(jax.random.fold_in(keys[9], 71), 0)
    global_blocks = jax.random.randint(keys[8], (GLOB,), 0, NBLK).astype(jnp.int32)
    return {"queries": queries, "key_heads": key_heads, "value_heads": value_heads, "output": output, "output_grad": output_grad, "log_totals": log_totals, "random_blocks": random_blocks, "window_width": window_width, "global_blocks": global_blocks}


def reference(queries, key_heads, value_heads, output, output_grad, log_totals, random_blocks, window_width, global_blocks):
    score_scale = HDIM ** -0.5
    head_group = HEADS // KV_HEADS
    kv_width = KV_HEADS * HDIM
    window_span = 2 * WIN + 1
    key_blocks = key_heads.reshape(NBLK, BLOCK, KV_HEADS, HDIM)
    value_blocks = value_heads.reshape(NBLK, BLOCK, KV_HEADS, HDIM)
    query_blocks = queries.reshape(NBLK, BLOCK, KV_HEADS, head_group, HDIM)
    grad_blocks = output_grad.reshape(NBLK, BLOCK, KV_HEADS, head_group, HDIM)
    output_blocks = output.reshape(NBLK, BLOCK, KV_HEADS, head_group, HDIM)
    lse_blocks = jnp.transpose(log_totals.reshape(KV_HEADS, head_group, NBLK, BLOCK), (2, 0, 1, 3))
    window_offsets = jnp.arange(-WIN, WIN + 1, dtype=jnp.int32)

    def round_random(values):
        kept = values[:window_span + GLOB]
        rounded = lax.optimization_barrier(values[window_span + GLOB:].astype(jnp.bfloat16)).astype(jnp.float32)
        return jnp.concatenate([kept, rounded], axis=0)

    def block_step(carry_sums, inputs):
        key_sums, value_sums = carry_sums
        block_index, query_tile, grad_tile, output_tile, lse_tile, random_row, width_value = inputs
        window_ids = block_index + window_offsets
        window_ok = (jnp.abs(window_offsets) <= width_value) & (window_ids >= 0) & (window_ids < NBLK)
        entry_ids = jnp.concatenate([window_ids, global_blocks.astype(jnp.int32), random_row.astype(jnp.int32)])
        safe_ids = jnp.clip(entry_ids, 0, NBLK - 1).astype(jnp.int32)
        live = jnp.concatenate([window_ok, jnp.ones((GLOB + RAND,), jnp.bool_)])
        key_tiles = key_blocks[safe_ids].astype(jnp.float32)
        value_tiles = value_blocks[safe_ids].astype(jnp.float32)
        query_float = query_tile.astype(jnp.float32)
        grad_float = grad_tile.astype(jnp.float32)
        delta_rows = jnp.sum(grad_float * output_tile.astype(jnp.float32), axis=-1)
        delta_heads = jnp.transpose(delta_rows, (1, 2, 0))
        scores = jnp.einsum('qcgd,jkcd->cgqjk', query_float, key_tiles) * score_scale
        probs = jnp.where(live[None, None, None, :, None], jnp.exp(scores - lse_tile[:, :, :, None, None]), 0.0)
        probs_half = lax.optimization_barrier(probs.astype(jnp.bfloat16)).astype(jnp.float32)
        value_entry = jnp.einsum('cgqjk,qcgd->jkcd', probs_half, grad_float)
        prob_grad = jnp.einsum('qcgd,jkcd->cgqjk', grad_float, value_tiles)
        score_grad = probs * (prob_grad - delta_heads[:, :, :, None, None])
        score_grad = lax.optimization_barrier(score_grad.astype(jnp.bfloat16)).astype(jnp.float32)
        query_part = jnp.einsum('cgqjk,jkcd->qcgd', score_grad, key_tiles) * score_scale
        key_entry = jnp.einsum('cgqjk,qcgd->jkcd', score_grad, query_float) * score_scale
        key_entry = round_random(key_entry.reshape(LIST, BLOCK, kv_width))
        value_entry = round_random(value_entry.reshape(LIST, BLOCK, kv_width))
        key_sums = key_sums.at[safe_ids].add(key_entry)
        value_sums = value_sums.at[safe_ids].add(value_entry)
        return (key_sums, value_sums), query_part.reshape(BLOCK, HEADS * HDIM).astype(jnp.bfloat16)

    zero_sums = jnp.zeros((NBLK, BLOCK, kv_width), jnp.float32)
    (key_sums, value_sums), query_grad = lax.scan(
        block_step, (zero_sums, zero_sums),
        (jnp.arange(NBLK, dtype=jnp.int32), query_blocks, grad_blocks, output_blocks, lse_blocks,
         random_blocks, window_width))
    return (query_grad.reshape(SEQ, HEADS * HDIM),
            key_sums.reshape(SEQ, kv_width).astype(jnp.bfloat16),
            value_sums.reshape(SEQ, kv_width).astype(jnp.bfloat16))
```

```python
import math

import jax
import jax.numpy as jnp
from jax import lax
from jax.experimental import pallas as pl
from jax.experimental.pallas import tpu as pltpu
from jax.sharding import PartitionSpec as P

MESH = pl.DeviceIdType.MESH
HDIM = 128
BLOCK = 128
NZ = 4
NY = 4
NI = 4
HALO = 32
GLOBAL = 48
SLOTS = 50
SCALE = HDIM ** (-0.5)
LOG2E = math.log2(math.e)
ZH = [(dz, dh) for dz in range(4) for dh in range(2) if (dz, dh) != (0, 0)]
BF = jnp.bfloat16
F32 = jnp.float32


def place():
    outer = lax.axis_index("outer")
    return outer // NY, lax.rem(outer, NY), lax.axis_index("inner"), lax.axis_index("head")


def device(z, y, i, h):
    return (z * NY + y, i, h)


def shifted(dz=0, dy=0, di=0, dh=0):
    z, y, i, h = place()
    return device(lax.rem(z + dz, NZ), lax.rem(y + dy, NY), lax.rem(i + di, NI), lax.rem(h + dh, 2))


def along(step):
    z, y, i, h = place()
    turn = lax.rem(y * NI + i + step + NY * NI, NY * NI)
    return device(z, turn // NI, lax.rem(turn, NI), h)


def peers():
    found = [shifted(dz=dz, dh=dh) for dz, dh in ZH]
    found += [shifted(dy=dy) for dy in range(1, NY)]
    found += [shifted(di=di) for di in range(1, NI)]
    found += [along(1), along(-1)]
    return found


def meet():
    barrier = pltpu.get_barrier_semaphore()
    found = peers()
    for one in found:
        pl.semaphore_signal(barrier, inc=1, device_id=one, device_id_type=MESH)
    pl.semaphore_wait(barrier, len(found))


def remote(src, dst, send, recv, to):
    return pltpu.make_async_remote_copy(
        src_ref=src, dst_ref=dst, send_sem=send, recv_sem=recv, device_id=to, device_id_type=MESH
    )


def columns(index, width):
    return pl.ds(pl.multiple_of(index * width, width), width)


def gather_kernel(
    glob_ref, q_ref, k_ref, v_ref, o_ref, g_ref, lse_ref, int_ref,
    qb, gb, kvu, stats, ints,
    og, sbuf, gsend, grecv,
    local_sem, kv_s, kv_r, q_s, q_r, st_s, st_r, it_s, it_r, ag_s, ag_r, hl_s, hl_r, gl_s, gl_r,
):
    z, y, i, h = place()
    loads = [
        pltpu.make_async_copy(o_ref, og.at[0], local_sem.at[0]),
        pltpu.make_async_copy(g_ref, og.at[1], local_sem.at[1]),
    ]
    own_col = columns(h * NZ + z, HDIM)
    own_slot = y * 8 + z * 2 + h
    keep = [
        pltpu.make_async_copy(k_ref.at[:, own_col], kvu.at[0, own_slot], local_sem.at[2]),
        pltpu.make_async_copy(v_ref.at[:, own_col], kvu.at[1, own_slot], local_sem.at[3]),
    ]
    stay = [
        pltpu.make_async_copy(q_ref.at[:, columns(z, 512)], qb.at[z], local_sem.at[4]),
        pltpu.make_async_copy(g_ref.at[:, columns(z, 512)], gb.at[z], local_sem.at[5]),
        pltpu.make_async_copy(int_ref, ints.at[z], local_sem.at[6]),
    ]
    for one in keep + loads + stay:
        one.start()
    meet()
    kv_copies = []
    for n, (dz, dh) in enumerate(ZH):
        to = shifted(dz=dz, dh=dh)
        col = columns(lax.rem(h + dh, 2) * NZ + lax.rem(z + dz, NZ), HDIM)
        for side, ref in enumerate((k_ref, v_ref)):
            kv_copies.append(
                remote(ref.at[:, col], kvu.at[side, own_slot], kv_s.at[2 * n + side], kv_r.at[2 * n + side], to)
            )
    for one in kv_copies:
        one.start()
    for one in loads:
        one.wait()
    picker = (
        lax.broadcasted_iota(jnp.int32, (8, 512), 1) // HDIM
        == lax.broadcasted_iota(jnp.int32, (8, 512), 0) - 4
    ).astype(BF)
    for c in range(NZ):
        prod = og[0, :, c * 512 : (c + 1) * 512].astype(F32) * og[1, :, c * 512 : (c + 1) * 512].astype(F32)
        high = prod.astype(BF)
        low = (prod - high.astype(F32)).astype(BF)
        dims = (((1,), (1,)), ((), ()))
        delta = lax.dot_general(picker, high, dims, preferred_element_type=F32)
        delta = delta + lax.dot_general(picker, low, dims, preferred_element_type=F32)
        sbuf[c] = jnp.concatenate([lse_ref[4 * c : 4 * c + 4, :] * LOG2E, delta[4:8]], axis=0)
    for one in keep:
        one.wait()
    for one in kv_copies:
        one.wait_recv()
    mine = pl.ds(pl.multiple_of(y * 8, 8), 8)
    ag_copies = []
    for dy in range(1, NY):
        to = shifted(dy=dy)
        for side in range(2):
            n = (dy - 1) * 2 + side
            ag_copies.append(remote(kvu.at[side, mine], kvu.at[side, mine], ag_s.at[n], ag_r.at[n], to))
    for one in ag_copies:
        one.start()
    halo_copies = []
    for n, step in enumerate((1, -1)):
        to = along(step)
        for side in range(2):
            halo_copies.append(
                remote(
                    kvu.at[side, mine],
                    kvu.at[side, pl.ds(HALO + 8 * n, 8)],
                    hl_s.at[2 * n + side],
                    hl_r.at[2 * n + side],
                    to,
                )
            )
    for one in halo_copies:
        one.start()
    rest = []
    for dz in range(1, NZ):
        to = shifted(dz=dz)
        c = lax.rem(z + dz, NZ)
        n = dz - 1
        rest.append(remote(q_ref.at[:, columns(c, 512)], qb.at[z], q_s.at[2 * n], q_r.at[2 * n], to))
        rest.append(remote(g_ref.at[:, columns(c, 512)], gb.at[z], q_s.at[2 * n + 1], q_r.at[2 * n + 1], to))
        rest.append(remote(sbuf.at[c], stats.at[z], st_s.at[n], st_r.at[n], to))
        rest.append(remote(int_ref, ints.at[z], it_s.at[n], it_r.at[n], to))
    for one in rest:
        one.start()
    own_stats = pltpu.make_async_copy(sbuf.at[z], stats.at[z], local_sem.at[7])
    own_stats.start()
    for one in ag_copies + halo_copies:
        one.wait_recv()
    for g in range(2):
        block = glob_ref[g]
        shard = block // 2
        slot = lax.rem(shard // NI, NY) * 8 + (shard // (NI * NY)) * 2 + lax.rem(block, 2)
        for side in range(2):
            gsend[side, g] = kvu[side, slot]
    gl_copies = []
    for di in range(1, NI):
        gl_copies.append(remote(gsend, grecv.at[di], gl_s.at[di - 1], gl_r.at[di - 1], shifted(di=di)))
    for one in gl_copies:
        one.start()
    grecv[0] = gsend[...]
    for one in gl_copies:
        one.wait_recv()
    for g in range(2):
        holder = lax.rem(glob_ref[g] // 2, NI)
        source = lax.rem(i - holder + NI, NI)
        for side in range(2):
            kvu[side, GLOBAL + g] = grecv[source, side, g]
    for one in kv_copies + ag_copies + halo_copies + gl_copies:
        one.wait_send()
    for one in rest + stay:
        one.wait()
    own_stats.wait()


def compute_kernel(
    glob_ref, ints, qb, gb, kvu, stats,
    dqb, rs, own, dhb, dgl,
    acc,
):
    z, y, i, h = place()
    turn = y * NI + i

    def clear(n, carry):
        acc[0, n] = jnp.zeros((BLOCK, HDIM), F32)
        acc[1, n] = jnp.zeros((BLOCK, HDIM), F32)
        return carry

    lax.fori_loop(0, SLOTS, clear, 0)

    def block_body(n, carry):
        zi = n // 2
        b = lax.rem(n, 2)
        rows = pl.ds(pl.multiple_of(b * BLOCK, BLOCK), BLOCK)
        query = jnp.concatenate([qb[zi, rows, j * HDIM : (j + 1) * HDIM] for j in range(4)], axis=0)
        grad = jnp.concatenate([gb[zi, rows, j * HDIM : (j + 1) * HDIM] for j in range(4)], axis=0)
        tile = stats[zi, :, rows]
        lse = jnp.concatenate([tile[j : j + 1] for j in range(4)], axis=1)
        delta = jnp.concatenate([tile[4 + j : 5 + j] for j in range(4)], axis=1)
        width = ints[zi, 0, 6 + b]
        block_id = (zi * (NY * NI) + turn) * 2 + b
        before = jnp.maximum(zi - (turn == 0).astype(jnp.int32), 0)
        after = jnp.minimum(zi + (turn == NY * NI - 1).astype(jnp.int32), NZ - 1)
        slots = []
        for e in range(5):
            at = b + e - 2
            slot = jnp.where(
                at < 0,
                HALO + before * 2 + at + 2,
                jnp.where(at >= 2, HALO + 8 + after * 2 + at - 2, y * 8 + zi * 2 + at),
            )
            target = block_id + e - 2
            ok = (abs(e - 2) <= width) & (target >= 0) & (target < 2 * NZ * NY * NI)
            slots.append((slot, jnp.where(ok, 0.0, 1e6).astype(F32)))
        for g in range(2):
            slots.append((GLOBAL + g, None))
        for r in range(3):
            block = ints[zi, 0, b * 3 + r]
            shard = block // 2
            slot = lax.rem(shard // NI, NY) * 8 + (shard // (NI * NY)) * 2 + lax.rem(block, 2)
            slots.append((slot, None))
        nt = (((1,), (1,)), ((), ()))
        tn = (((0,), (0,)), ((), ()))
        total = jnp.zeros((HDIM, 512), F32)
        for p in range(5):
            pair = slots[2 * p : 2 * p + 2]
            keys = jnp.concatenate([kvu[0, s] for s, _ in pair], axis=0)
            values = jnp.concatenate([kvu[1, s] for s, _ in pair], axis=0)
            scores = lax.dot_general(keys, query, nt, preferred_element_type=F32) * (SCALE * LOG2E)
            lses = [lse if off is None else lse + off for _, off in pair]
            scores = jnp.concatenate(
                [scores[:BLOCK] - lses[0], scores[BLOCK:] - lses[1]], axis=0
            )
            probs = jnp.exp2(scores)
            prob_grad = lax.dot_general(values, grad, nt, preferred_element_type=F32)
            score_grad = (probs * (prob_grad - delta)).astype(BF)
            value_entry = jnp.dot(probs.astype(BF), grad, preferred_element_type=F32)
            key_entry = jnp.dot(score_grad, query, preferred_element_type=F32)
            total = total + lax.dot_general(keys, score_grad, tn, preferred_element_type=F32)
            for k in range(2):
                s = pair[k][0]
                acc[0, s] += key_entry[k * BLOCK : (k + 1) * BLOCK]
                acc[1, s] += value_entry[k * BLOCK : (k + 1) * BLOCK]
        done = (jnp.transpose(total) * SCALE).astype(BF)
        for j in range(4):
            dqb[zi, rows, j * HDIM : (j + 1) * HDIM] = done[j * BLOCK : (j + 1) * BLOCK]
        return carry

    lax.fori_loop(0, 8, block_body, 0)
    for side in range(2):
        factor = SCALE if side == 0 else 1.0

        def give(n, carry):
            rs[n // 8, side, lax.rem(n, 8)] = (acc[side, n] * factor).astype(BF)
            return carry

        lax.fori_loop(0, 32, give, 0)

        def give_halo(n, carry):
            dhb[n // 8, side, lax.rem(n, 8)] = (acc[side, HALO + n] * factor).astype(BF)
            return carry

        lax.fori_loop(0, 16, give_halo, 0)

        def give_own(n, carry):
            own[side, n] = acc[side, y * 8 + n] * factor
            return carry

        lax.fori_loop(0, 8, give_own, 0)
        for g in range(2):
            dgl[side, g] = (acc[side, GLOBAL + g] * factor).astype(BF)


def return_kernel(
    glob_ref, dqb, rs, own, dhb, dgl,
    dq, dk, dv,
    rsr, hr, g1, g2s, g2r, g3s, g3r, acc, outb,
    local_sem, dq_s, dq_r, rs_s, rs_r, hl_s, hl_r, g1_s, g1_r, g2_s, g2_r, g3_s, g3_r, kv_s, kv_r,
):
    z, y, i, h = place()
    stay = pltpu.make_async_copy(dqb.at[z], dq.at[:, columns(z, 512)], local_sem.at[0])
    stay.start()
    meet()
    g1_copies = []
    for di in range(1, NI):
        part = lax.rem(i + di, NI)
        g1_copies.append(remote(dgl.at[part], g1.at[di], g1_s.at[di - 1], g1_r.at[di - 1], shifted(di=di)))
    rs_copies = []
    for dy in range(1, NY):
        to = lax.rem(y + dy, NY)
        rs_copies.append(remote(rs.at[to], rsr.at[dy - 1], rs_s.at[dy - 1], rs_r.at[dy - 1], shifted(dy=dy)))
    hl_copies = [
        remote(dhb.at[0], hr.at[0], hl_s.at[0], hl_r.at[0], along(-1)),
        remote(dhb.at[1], hr.at[1], hl_s.at[1], hl_r.at[1], along(1)),
    ]
    dq_copies = []
    for dz in range(1, NZ):
        to = lax.rem(z + dz, NZ)
        dq_copies.append(
            remote(dqb.at[to], dq.at[:, columns(z, 512)], dq_s.at[dz - 1], dq_r.at[dz - 1], shifted(dz=dz))
        )
    for one in g1_copies + rs_copies + hl_copies + dq_copies:
        one.start()
    for one in g1_copies:
        one.wait_recv()
    partial = dgl[i].astype(F32)
    for di in range(1, NI):
        partial = partial + g1[di].astype(F32)
    g2s[...] = partial.astype(BF)
    g2_copies = [
        remote(g2s, g2r.at[dy - 1], g2_s.at[dy - 1], g2_r.at[dy - 1], shifted(dy=dy)) for dy in range(1, NY)
    ]
    for one in g2_copies:
        one.start()
    for one in g2_copies:
        one.wait_recv()
    for dy in range(1, NY):
        partial = partial + g2r[dy - 1].astype(F32)
    g3s[...] = partial.astype(BF)
    g3r[i] = g3s[...]
    g3_copies = [
        remote(g3s, g3r.at[i], g3_s.at[di - 1], g3_r.at[di - 1], shifted(di=di)) for di in range(1, NI)
    ]
    for one in g3_copies:
        one.start()
    for one in g3_copies:
        one.wait_recv()
    for one in hl_copies:
        one.wait_recv()
    turn = y * NI + i

    def begin(n, carry):
        zi = n // 2
        b = lax.rem(n, 2)
        block = (zi * (NY * NI) + turn) * 2 + b
        for side in range(2):
            total = own[side, n]
            total = total + hr[0, side, n].astype(F32) + hr[1, side, n].astype(F32)
            for g in range(2):
                hit = (jnp.zeros((BLOCK, HDIM), jnp.int32) + glob_ref[g]) == block
                both = jnp.concatenate([g3r[2 * side, g], g3r[2 * side + 1, g]], axis=0).astype(F32)
                total = total + jnp.where(hit, both, 0.0)
            acc[side, n] = total
        return carry

    lax.fori_loop(0, 8, begin, 0)
    for one in rs_copies:
        one.wait_recv()

    def finish(n, carry):
        for side in range(2):
            total = acc[side, n]
            for dy in range(NY - 1):
                total = total + rsr[dy, side, n].astype(F32)
            outb[side, n] = total.astype(BF)
        return carry

    lax.fori_loop(0, 8, finish, 0)
    col = columns(h * NZ + z, HDIM)
    mine = z * 2 + h
    home = [
        pltpu.make_async_copy(outb.at[0, mine], dk.at[:, col], local_sem.at[1]),
        pltpu.make_async_copy(outb.at[1, mine], dv.at[:, col], local_sem.at[2]),
    ]
    for one in home:
        one.start()
    kv_copies = []
    for n, (dz, dh) in enumerate(ZH):
        to = shifted(dz=dz, dh=dh)
        slot = lax.rem(z + dz, NZ) * 2 + lax.rem(h + dh, 2)
        for side, ref in enumerate((dk, dv)):
            kv_copies.append(
                remote(outb.at[side, slot], ref.at[:, col], kv_s.at[2 * n + side], kv_r.at[2 * n + side], to)
            )
    for one in kv_copies:
        one.start()
    for one in home + [stay] + kv_copies + dq_copies:
        one.wait()
    for one in g1_copies + rs_copies + hl_copies + g2_copies + g3_copies:
        one.wait_send()


ANY = pl.BlockSpec(memory_space=pl.ANY)
VMEM = pl.BlockSpec(memory_space=pltpu.VMEM)
SMEM = pl.BlockSpec(memory_space=pltpu.SMEM)
DMA = pltpu.SemaphoreType.DMA


def params(collective_id=None):
    if collective_id is None:
        return pltpu.CompilerParams(vmem_limit_bytes=40 * 2**20)
    return pltpu.CompilerParams(
        collective_id=collective_id, has_side_effects=True, vmem_limit_bytes=40 * 2**20
    )


def on_device(
    queries, key_heads, value_heads, output, output_grad, log_totals, random_blocks, window_width, global_blocks
):
    row = jnp.pad(jnp.concatenate([random_blocks.reshape(-1), window_width]), (0, 120))
    listed = jnp.broadcast_to(row[None], (8, 128))
    shape = jax.ShapeDtypeStruct
    qb, gb, kvu, stats, ints = pl.pallas_call(
        gather_kernel,
        out_shape=(
            shape((NZ, 256, 512), BF),
            shape((NZ, 256, 512), BF),
            shape((2, SLOTS, BLOCK, HDIM), BF),
            shape((NZ, 8, 256), F32),
            shape((NZ, 8, 128), jnp.int32),
        ),
        in_specs=[SMEM, ANY, ANY, ANY, ANY, ANY, VMEM, ANY],
        out_specs=(ANY, ANY, VMEM, VMEM, ANY),
        scratch_shapes=[
            pltpu.VMEM((2, 256, 2048), BF),
            pltpu.VMEM((NZ, 8, 256), F32),
            pltpu.VMEM((2, 2, BLOCK, HDIM), BF),
            pltpu.VMEM((NI, 2, 2, BLOCK, HDIM), BF),
            DMA((8,)),
            DMA((14,)), DMA((14,)),
            DMA((6,)), DMA((6,)),
            DMA((3,)), DMA((3,)),
            DMA((3,)), DMA((3,)),
            DMA((6,)), DMA((6,)),
            DMA((4,)), DMA((4,)),
            DMA((3,)), DMA((3,)),
        ],
        compiler_params=params(0),
        name="gather",
    )(global_blocks, queries, key_heads, value_heads, output, output_grad, log_totals, listed)
    dqb, rs, own, dhb, dgl = pl.pallas_call(
        compute_kernel,
        out_shape=(
            shape((NZ, 256, 512), BF),
            shape((NY, 2, 8, BLOCK, HDIM), BF),
            shape((2, 8, BLOCK, HDIM), F32),
            shape((2, 2, 8, BLOCK, HDIM), BF),
            shape((2, 2, BLOCK, HDIM), BF),
        ),
        in_specs=[SMEM, SMEM, VMEM, VMEM, VMEM, VMEM],
        out_specs=(VMEM,) * 5,
        scratch_shapes=[pltpu.VMEM((2, SLOTS, BLOCK, HDIM), F32)],
        compiler_params=params(),
        name="compute",
    )(global_blocks, ints, qb, gb, kvu, stats)
    parts = jnp.transpose(dgl.reshape(2, 2, 2, 64, HDIM), (0, 2, 1, 3, 4)).reshape(4, 2, 64, HDIM)
    return pl.pallas_call(
        return_kernel,
        out_shape=(
            shape((256, 2048), BF),
            shape((BLOCK, 1024), BF),
            shape((BLOCK, 1024), BF),
        ),
        in_specs=[SMEM, ANY, ANY, VMEM, ANY, VMEM],
        out_specs=(ANY, ANY, ANY),
        scratch_shapes=[
            pltpu.VMEM((NY - 1, 2, 8, BLOCK, HDIM), BF),
            pltpu.VMEM((2, 2, 8, BLOCK, HDIM), BF),
            pltpu.VMEM((NI, 2, 64, HDIM), BF),
            pltpu.VMEM((2, 64, HDIM), BF),
            pltpu.VMEM((NY - 1, 2, 64, HDIM), BF),
            pltpu.VMEM((2, 64, HDIM), BF),
            pltpu.VMEM((NI, 2, 64, HDIM), BF),
            pltpu.VMEM((2, 8, BLOCK, HDIM), F32),
            pltpu.VMEM((2, 8, BLOCK, HDIM), BF),
            DMA((3,)),
            DMA((3,)), DMA((3,)),
            DMA((3,)), DMA((3,)),
            DMA((2,)), DMA((2,)),
            DMA((3,)), DMA((3,)),
            DMA((3,)), DMA((3,)),
            DMA((3,)), DMA((3,)),
            DMA((14,)), DMA((14,)),
        ],
        compiler_params=params(1),
        name="give_back",
    )(global_blocks, dqb, rs, own, dhb, parts)


def solution(mesh):
    placed = (
        P(("outer", "inner"), "head"),
        P(("outer", "inner", "head"), None),
        P(("outer", "inner", "head"), None),
        P(("outer", "inner"), "head"),
        P(("outer", "inner"), "head"),
        P("head", ("outer", "inner")),
        P(("outer", "inner"), None),
        P(("outer", "inner")),
        P(),
    )
    return jax.shard_map(
        on_device,
        mesh=mesh,
        in_specs=placed,
        out_specs=(
            P(("outer", "inner"), "head"),
            P(("outer", "inner", "head"), None),
            P(("outer", "inner", "head"), None),
        ),
        check_vma=False,
    )
```

```python
import math

import jax
import jax.numpy as jnp
from jax import lax
from jax.experimental import pallas as pl
from jax.experimental.pallas import tpu as pltpu
from jax.sharding import PartitionSpec as P

MESH = pl.DeviceIdType.MESH
HDIM = 128
BLOCK = 128
N = 4
SCALE = HDIM ** (-0.5)
LOG2E = math.log2(math.e)
YH = [(dy, dh) for dy in range(4) for dh in range(2) if (dy, dh) != (0, 0)]
BF = jnp.bfloat16
F32 = jnp.float32
I32 = jnp.int32
NT = (((1,), (1,)), ((), ()))
TN = (((0,), (0,)), ((), ()))


def place():
    outer = lax.axis_index("outer")
    return outer // N, lax.rem(outer, N), lax.axis_index("inner"), lax.axis_index("head")


def device(z, y, i, h):
    return (z * N + y, i, h)


def shifted(dz=0, dy=0, di=0, dh=0):
    z, y, i, h = place()
    return device(lax.rem(z + dz, N), lax.rem(y + dy, N), lax.rem(i + di, N), lax.rem(h + dh, 2))


def following(shard):
    z, y, i, h = place()
    wrap = (i == N - 1).astype(I32)
    spot = lax.rem(shard + wrap, N)
    cross = wrap * jnp.where(shard == N - 1, 1, 0)
    return device(lax.rem(z + cross, N), y, lax.rem(i + 1, N), h), spot


def preceding(shard):
    z, y, i, h = place()
    wrap = (i == 0).astype(I32)
    spot = lax.rem(shard - wrap + N, N)
    cross = wrap * jnp.where(shard == 0, 1, 0)
    return device(lax.rem(z - cross + N, N), y, lax.rem(i + N - 1, N), h), spot


def meet():
    barrier = pltpu.get_barrier_semaphore()
    found = [shifted(dy=dy, dh=dh) for dy, dh in YH]
    found += [shifted(dz=dz) for dz in range(1, N)]
    found += [shifted(di=di) for di in range(1, N)]
    found += [following(N - 1)[0], preceding(0)[0]]
    for one in found:
        pl.semaphore_signal(barrier, inc=1, device_id=one, device_id_type=MESH)
    pl.semaphore_wait(barrier, len(found))


def remote(src, dst, send, recv, to):
    return pltpu.make_async_remote_copy(
        src_ref=src, dst_ref=dst, send_sem=send, recv_sem=recv, device_id=to, device_id_type=MESH
    )


def columns(index, width):
    return pl.ds(pl.multiple_of(index * width, width), width)


def offset_of(k):
    if isinstance(k, int):
        return (0, 1, 3, 2)[k]
    return k + (k == 2).astype(I32) - (k == 3).astype(I32)


def block_slot(block):
    shard = block // 2
    return (shard // (N * N)) * 8 + lax.rem(shard // N, N) * 2 + lax.rem(block, 2)


def fused(
    glob_ref, rand_ref, width_ref, q_ref, k_ref, v_ref, o_ref, g_ref, lse_ref,
    dq, dk, dv,
    og, lseb, sbuf, intb, intr, ints, stats, qb, gb, kvu, hal, gsend, grecv,
    dqt, acc, dhb, hrn, hrp, ent, spots, rsb, rsr, gacc, dglb, g1r, g2s, g2r, g3r, dqb, outb,
    loc, kv_s, kv_r, q_s, q_r, st_s, st_r, it_s, it_r, ag_s, ag_r, hn_s, hn_r, hp_s, hp_r, gl_s, gl_r,
    dn_s, dn_r, dp_s, dp_r, rs_s, rs_r, g1_s, g1_r, g2_s, g2_r, g3_s, g3_r, dq_s, dq_r, out_s, out_r,
):
    z, y, i, h = place()
    own_slot = z * 8 + y * 2 + h
    own_col = columns(h * N + y, HDIM)
    loads = [
        pltpu.make_async_copy(o_ref, og.at[0], loc.at[0]),
        pltpu.make_async_copy(g_ref, og.at[1], loc.at[1]),
        pltpu.make_async_copy(lse_ref, lseb, loc.at[2]),
    ]
    keep = [
        pltpu.make_async_copy(k_ref.at[:, own_col], kvu.at[own_slot, 0], loc.at[3]),
        pltpu.make_async_copy(v_ref.at[:, own_col], kvu.at[own_slot, 1], loc.at[4]),
    ]
    stay = [
        pltpu.make_async_copy(q_ref.at[:, columns(y, 512)], qb.at[y], loc.at[5]),
        pltpu.make_async_copy(g_ref.at[:, columns(y, 512)], gb.at[y], loc.at[6]),
    ]
    for one in keep + loads + stay:
        one.start()
    lane = lax.broadcasted_iota(I32, (8, 128), 1)
    row = jnp.zeros((8, 128), I32)
    for b in range(2):
        for r in range(3):
            row = jnp.where(lane == b * 3 + r, rand_ref[b, r], row)
        row = jnp.where(lane == 6 + b, width_ref[b], row)
    intb[...] = row
    meet()

    it_copies = [
        remote(intb, intr.at[y], it_s.at[dy - 1], it_r.at[dy - 1], shifted(dy=dy)) for dy in range(1, N)
    ]
    kv_copies = {}
    for n, (dy, dh) in enumerate(YH):
        to = shifted(dy=dy, dh=dh)
        col = columns(lax.rem(h + dh, 2) * N + lax.rem(y + dy, N), HDIM)
        for side, ref in enumerate((k_ref, v_ref)):
            kv_copies[dy, dh, side] = remote(
                ref.at[:, col], kvu.at[own_slot, side], kv_s.at[2 * n + side], kv_r.at[2 * n + side], to
            )
    for key in sorted(kv_copies, key=lambda s: ((0, 1, 3, 2)[s[0]], s[1], s[2])):
        kv_copies[key].start()
    for one in it_copies:
        one.start()
    intr[y] = row

    for one in loads:
        one.wait()
    picker = (
        lax.broadcasted_iota(I32, (8, 512), 1) // HDIM == lax.broadcasted_iota(I32, (8, 512), 0) - 4
    ).astype(BF)
    for c in range(N):
        prod = og[0, :, c * 512 : (c + 1) * 512].astype(F32) * og[1, :, c * 512 : (c + 1) * 512].astype(F32)
        high = prod.astype(BF)
        low = (prod - high.astype(F32)).astype(BF)
        delta = lax.dot_general(picker, high, NT, preferred_element_type=F32)
        delta = delta + lax.dot_general(picker, low, NT, preferred_element_type=F32)
        sbuf[c] = jnp.concatenate([lseb[4 * c : 4 * c + 4, :] * LOG2E, delta[4:8]], axis=0)
    st_copies = [
        remote(sbuf.at[lax.rem(y + dy, N)], stats.at[y], st_s.at[dy - 1], st_r.at[dy - 1], shifted(dy=dy))
        for dy in range(1, N)
    ]
    for one in st_copies:
        one.start()
    own_stats = pltpu.make_async_copy(sbuf.at[y], stats.at[y], loc.at[7])
    own_stats.start()
    for one in keep:
        one.wait()

    ag_copies, hn_copies, hp_copies = [], [], []
    for dy in (0, 1, 3, 2):
        shard = lax.rem(y - dy + N, N)
        for dh in range(2):
            for side in range(2):
                if (dy, dh) != (0, 0):
                    kv_copies[dy, dh, side].wait_recv()
        here = pl.ds(pl.multiple_of(z * 8 + shard * 2, 2), 2)
        for dz in range(1, N):
            n = dy * 3 + dz - 1
            ag_copies.append(remote(kvu.at[here], kvu.at[here], ag_s.at[n], ag_r.at[n], shifted(dz=dz)))
            ag_copies[-1].start()
        to, spot = following(shard)
        hn_copies.append(remote(kvu.at[here], hal.at[0, spot], hn_s.at[dy], hn_r.at[spot], to))
        hn_copies[-1].start()
        to, spot = preceding(shard)
        hp_copies.append(remote(kvu.at[here], hal.at[1, spot], hp_s.at[dy], hp_r.at[spot], to))
        hp_copies[-1].start()
    q_copies = {}
    for dy in (1, 3, 2):
        c = lax.rem(y + dy, N)
        for side, (ref, dst) in enumerate(((q_ref, qb), (g_ref, gb))):
            n = 2 * (dy - 1) + side
            q_copies[dy, side] = remote(
                ref.at[:, columns(c, 512)], dst.at[y], q_s.at[n], q_r.at[n], shifted(dy=dy)
            )
            q_copies[dy, side].start()

    for one in it_copies + st_copies:
        one.wait_recv()
    own_stats.wait()
    to_scalar = pltpu.make_async_copy(intr, ints, loc.at[8])
    to_scalar.start()
    to_scalar.wait()
    for shard in range(N):
        ent[shard, 0] = jnp.zeros((2, BLOCK, HDIM), BF)
    for b in range(2):
        dqt[6 + b] = jnp.zeros((HDIM, 512), F32)
    for g in range(2):
        for side in range(2):
            gacc[g, side] = jnp.zeros((BLOCK, HDIM), F32)

    def find(slot, carry):
        for shard in range(N):
            spot = 0
            for r in range(6):
                spot = jnp.where(block_slot(ints[shard, 0, r]) == slot, r + 1, spot)
            spots[slot, shard] = spot
        return carry

    lax.fori_loop(0, 32, find, 0)

    def load_block(shard, b):
        rows = slice(b * BLOCK, (b + 1) * BLOCK)
        query = jnp.concatenate([qb[shard, rows, j * HDIM : (j + 1) * HDIM] for j in range(4)], axis=0)
        grad = jnp.concatenate([gb[shard, rows, j * HDIM : (j + 1) * HDIM] for j in range(4)], axis=0)
        tile = stats[shard, :, rows]
        lse = jnp.concatenate([tile[j : j + 1] for j in range(4)], axis=1)
        delta = jnp.concatenate([tile[4 + j : 5 + j] for j in range(4)], axis=1)
        return query, grad, lse, delta

    def attend(pairs, lses, query, grad, delta):
        count = len(pairs)
        keys = jnp.concatenate([k for k, _ in pairs], axis=0)
        values = jnp.concatenate([v for _, v in pairs], axis=0)
        scores = lax.dot_general(keys, query, NT, preferred_element_type=F32) * (SCALE * LOG2E)
        scores = jnp.concatenate([scores[k * BLOCK : (k + 1) * BLOCK] - lses[k] for k in range(count)], axis=0)
        probs = jnp.exp2(scores)
        prob_grad = lax.dot_general(values, grad, NT, preferred_element_type=F32)
        score_grad = (probs * (prob_grad - delta)).astype(BF)
        value_entry = jnp.dot(probs.astype(BF), grad, preferred_element_type=F32)
        key_entry = jnp.dot(score_grad, query, preferred_element_type=F32)
        turned = lax.dot_general(keys, score_grad, TN, preferred_element_type=F32)
        cut = [slice(k * BLOCK, (k + 1) * BLOCK) for k in range(count)]
        return [key_entry[c] for c in cut], [value_entry[c] for c in cut], turned

    def window(k, add):
        shard = lax.rem(y - offset_of(k) + N, N)
        for b in range(2):
            query, grad, lse, delta = load_block(shard, b)
            width = ints[shard, 0, 6 + b]
            block_id = ((z * N + shard) * N + i) * 2 + b
            total = None
            for group in ((0, 1), (2, 3), (4,)):
                pairs, lses = [], []
                for e in group:
                    at = b + e - 2
                    if at < 0:
                        pairs.append((hal[0, shard, at + 2, 0], hal[0, shard, at + 2, 1]))
                    elif at >= 2:
                        pairs.append((hal[1, shard, at - 2, 0], hal[1, shard, at - 2, 1]))
                    else:
                        slot = z * 8 + shard * 2 + at
                        pairs.append((kvu[slot, 0], kvu[slot, 1]))
                    target = block_id + e - 2
                    ok = (abs(e - 2) <= width) & (target >= 0) & (target < 128)
                    lses.append(lse + jnp.where(ok, 0.0, 1e6).astype(F32))
                dks, dvs, turned = attend(pairs, lses, query, grad, delta)
                total = turned if total is None else total + turned
                for e, dk_e, dv_e in zip(group, dks, dvs):
                    at = b + e
                    if b == 0 or at == 5:
                        acc[shard, at, 0] = dk_e
                        acc[shard, at, 1] = dv_e
                    else:
                        acc[shard, at, 0] += dk_e
                        acc[shard, at, 1] += dv_e
            if add:
                dqt[2 * k + b] += total
            else:
                dqt[2 * k + b] = total
        for n, start in enumerate((0, 4)):
            for b in range(2):
                dhb[n, shard, b, 0] = (acc[shard, start + b, 0] * SCALE).astype(BF)
                dhb[n, shard, b, 1] = acc[shard, start + b, 1].astype(BF)
        to, spot = preceding(shard)
        remote(dhb.at[0, shard], hrn.at[spot], dn_s.at[shard], dn_r.at[spot], to).start()
        to, spot = following(shard)
        remote(dhb.at[1, shard], hrp.at[spot], dp_s.at[shard], dp_r.at[spot], to).start()

    def wait_queries(k):
        dy = offset_of(k)
        for side, (ref, dst) in enumerate(((q_ref, qb), (g_ref, gb))):
            n = 2 * (dy - 1) + side
            remote(
                ref.at[:, columns(y, 512)], dst.at[y], q_s.at[n], q_r.at[n], shifted(dy=1)
            ).wait_recv()

    for one in stay:
        one.wait()
    for shard in range(N):
        remote(hal.at[0, shard], hal.at[0, shard], hn_s.at[shard], hn_r.at[shard], shifted(di=1)).wait_recv()
        remote(hal.at[1, shard], hal.at[1, shard], hp_s.at[shard], hp_r.at[shard], shifted(di=1)).wait_recv()

    def early(k, carry):
        @pl.when(k > 0)
        def _():
            wait_queries(k)

        window(k, False)
        return carry

    lax.fori_loop(0, 3, early, 0)

    for one in ag_copies:
        one.wait_recv()
    for g in range(2):
        gsend[g] = kvu[block_slot(glob_ref[g])]
    gl_copies = [
        remote(gsend, grecv.at[di], gl_s.at[di - 1], gl_r.at[di - 1], shifted(di=di)) for di in range(1, N)
    ]
    for one in gl_copies:
        one.start()
    grecv[0] = gsend[...]

    def random(k, carry):
        @pl.when(k == 3)
        def _():
            wait_queries(k)

        shard = lax.rem(y - offset_of(k) + N, N)
        for b in range(2):
            query, grad, lse, delta = load_block(shard, b)
            total = None
            for group in ((0, 1), (2,)):
                slots = [block_slot(ints[shard, 0, b * 3 + r]) for r in group]
                pairs = [(kvu[s, 0], kvu[s, 1]) for s in slots]
                dks, dvs, turned = attend(pairs, [lse] * len(group), query, grad, delta)
                total = turned if total is None else total + turned
                for r, dk_e, dv_e in zip(group, dks, dvs):
                    ent[shard, 1 + b * 3 + r, 0] = (dk_e * SCALE).astype(BF)
                    ent[shard, 1 + b * 3 + r, 1] = dv_e.astype(BF)
            dqt[2 * k + b] += total
        return carry

    lax.fori_loop(0, N, random, 0)

    def named(slot):
        total = None
        for shard in range(N):
            one = ent[shard, spots[slot, shard]].astype(F32)
            total = one if total is None else total + one
        return total

    rs_copies = []
    for dy in range(N):
        shard = lax.rem(y + dy, N)
        for dz in range(1, N):
            to = lax.rem(z + dz, N)

            def fill(b, carry, to=to, shard=shard, dz=dz):
                rsb[dz - 1, shard, b] = named(to * 8 + shard * 2 + b).astype(BF)
                return carry

            lax.fori_loop(0, 2, fill, 0)
            n = dy * 3 + dz - 1
            rs_copies.append(
                remote(rsb.at[dz - 1, shard], rsr.at[dz - 1, shard], rs_s.at[n], rs_r.at[n], shifted(dz=dz))
            )
            rs_copies[-1].start()

    for one in gl_copies:
        one.wait_recv()
    globe = []
    for g in range(2):
        source = lax.rem(i - lax.rem(glob_ref[g] // 2, N) + N, N)
        globe.append(source)

    def dq_copy(k):
        dy = offset_of(k)
        shard = lax.rem(y - dy + N, N)
        return remote(
            dqb.at[shard], dq.at[:, columns(y, 512)], dq_s.at[dy - 1], dq_r.at[dy - 1], device(z, shard, i, h)
        )

    dq_home = pltpu.make_async_copy(dqb.at[y], dq.at[:, columns(y, 512)], loc.at[9])

    def whole(k, carry):
        shard = lax.rem(y - offset_of(k) + N, N)
        for b in range(2):
            query, grad, lse, delta = load_block(shard, b)
            pairs = [(grecv[globe[g], g, 0], grecv[globe[g], g, 1]) for g in range(2)]
            dks, dvs, turned = attend(pairs, [lse] * 2, query, grad, delta)
            for g in range(2):
                gacc[g, 0] += dks[g]
                gacc[g, 1] += dvs[g]
            done = (jnp.transpose(dqt[2 * k + b] + turned) * SCALE).astype(BF)
            for j in range(4):
                dqb[shard, b * BLOCK : (b + 1) * BLOCK, j * HDIM : (j + 1) * HDIM] = done[
                    j * BLOCK : (j + 1) * BLOCK
                ]

        @pl.when(k == 0)
        def _():
            dq_home.start()

        @pl.when(k > 0)
        def _():
            dq_copy(k).start()

        return carry

    def late(k, carry):
        window(k, True)
        return carry

    lax.fori_loop(3, 4, late, 0)
    lax.fori_loop(0, N, whole, 0)

    for g in range(2):
        dglb[2 * g] = (gacc[g, 0] * SCALE).astype(BF)
        dglb[2 * g + 1] = gacc[g, 1].astype(BF)
    g1_copies = [
        remote(dglb.at[lax.rem(i + di, N)], g1r.at[di - 1], g1_s.at[di - 1], g1_r.at[di - 1], shifted(di=di))
        for di in range(1, N)
    ]
    for one in g1_copies:
        one.start()
    for one in g1_copies:
        one.wait_recv()
    partial = dglb[i].astype(F32)
    for n in range(3):
        partial = partial + g1r[n].astype(F32)
    g2s[0] = partial.astype(BF)
    g2_copies = [
        remote(g2s.at[0], g2r.at[dz - 1], g2_s.at[dz - 1], g2_r.at[dz - 1], shifted(dz=dz)) for dz in range(1, N)
    ]
    for one in g2_copies:
        one.start()
    for one in g2_copies:
        one.wait_recv()
    for n in range(3):
        partial = partial + g2r[n].astype(F32)
    g2s[1] = partial.astype(BF)
    g3r[i] = g2s[1]
    g3_copies = [
        remote(g2s.at[1], g3r.at[i], g3_s.at[di - 1], g3_r.at[di - 1], shifted(di=di)) for di in range(1, N)
    ]
    for one in g3_copies:
        one.start()
    for one in g3_copies:
        one.wait_recv()
    for shard in range(N):
        remote(dhb.at[0, shard], hrn.at[shard], dn_s.at[shard], dn_r.at[shard], shifted(di=1)).wait_recv()
        remote(dhb.at[1, shard], hrp.at[shard], dp_s.at[shard], dp_r.at[shard], shifted(di=1)).wait_recv()

    out_copies, home = [], []
    for dy in range(N):
        shard = lax.rem(y + dy, N)
        for dz in range(1, N):
            rs_copies[dy * 3 + dz - 1].wait_recv()

        def close(b, carry, shard=shard):
            block_id = ((z * N + shard) * N + i) * 2 + b
            extra = named(z * 8 + shard * 2 + b)
            for side in range(2):
                total = acc[shard, 2 + b, side] * (SCALE if side == 0 else 1.0) + extra[side]
                total = total + hrn[shard, b, side].astype(F32) + hrp[shard, b, side].astype(F32)
                for n in range(3):
                    total = total + rsr[n, shard, b, side].astype(F32)
                for g in range(2):
                    hit = (jnp.zeros((BLOCK, HDIM), I32) + glob_ref[g]) == block_id
                    total = total + jnp.where(hit, g3r[2 * g + side].astype(F32), 0.0)
                outb[shard, b, side] = total.astype(BF)
            return carry

        lax.fori_loop(0, 2, close, 0)
        for dh in range(2):
            b = lax.rem(h + dh, 2)
            for side, ref in enumerate((dk, dv)):
                if (dy, dh) == (0, 0):
                    home.append(
                        pltpu.make_async_copy(outb.at[shard, b, side], ref.at[:, own_col], loc.at[10 + side])
                    )
                    home[-1].start()
                else:
                    n = 2 * YH.index((dy, dh)) + side
                    out_copies.append(
                        remote(
                            outb.at[shard, b, side],
                            ref.at[:, own_col],
                            out_s.at[n],
                            out_r.at[n],
                            shifted(dy=dy, dh=dh),
                        )
                    )
                    out_copies[-1].start()
    for one in out_copies + home + [dq_home]:
        one.wait()
    for k in range(1, N):
        dq_copy(k).wait()
    for one in list(kv_copies.values()) + list(q_copies.values()) + it_copies + st_copies:
        one.wait_send()
    for one in ag_copies + hn_copies + hp_copies + gl_copies + rs_copies + g1_copies + g2_copies + g3_copies:
        one.wait_send()
    for shard in range(N):
        remote(dhb.at[0, shard], hrn.at[shard], dn_s.at[shard], dn_r.at[shard], shifted(di=1)).wait_send()
        remote(dhb.at[1, shard], hrp.at[shard], dp_s.at[shard], dp_r.at[shard], shifted(di=1)).wait_send()


HBM = pl.BlockSpec(memory_space=pltpu.HBM)
SMEM = pl.BlockSpec(memory_space=pltpu.SMEM)
DMA = pltpu.SemaphoreType.DMA


def on_device(
    queries, key_heads, value_heads, output, output_grad, log_totals, random_blocks, window_width, global_blocks
):
    shape = jax.ShapeDtypeStruct
    tile = (BLOCK, HDIM)
    twice = lambda n: [DMA((n,)), DMA((n,))]
    return pl.pallas_call(
        fused,
        out_shape=(
            shape((256, 2048), BF),
            shape((BLOCK, 1024), BF),
            shape((BLOCK, 1024), BF),
        ),
        in_specs=[SMEM, SMEM, SMEM] + [HBM] * 6,
        out_specs=(HBM, HBM, HBM),
        scratch_shapes=[
            pltpu.VMEM((2, 256, 2048), BF),
            pltpu.VMEM((16, 256), F32),
            pltpu.VMEM((N, 8, 256), F32),
            pltpu.VMEM((8, 128), I32),
            pltpu.VMEM((N, 8, 128), I32),
            pltpu.SMEM((N, 8, 128), I32),
            pltpu.VMEM((N, 8, 256), F32),
            pltpu.VMEM((N, 256, 512), BF),
            pltpu.VMEM((N, 256, 512), BF),
            pltpu.VMEM((32, 2) + tile, BF),
            pltpu.VMEM((2, N, 2, 2) + tile, BF),
            pltpu.VMEM((2, 2) + tile, BF),
            pltpu.VMEM((N, 2, 2) + tile, BF),
            pltpu.VMEM((8, HDIM, 512), F32),
            pltpu.VMEM((N, 6, 2) + tile, F32),
            pltpu.VMEM((2, N, 2, 2) + tile, BF),
            pltpu.VMEM((N, 2, 2) + tile, BF),
            pltpu.VMEM((N, 2, 2) + tile, BF),
            pltpu.VMEM((N, 7, 2) + tile, BF),
            pltpu.SMEM((32, N), I32),
            pltpu.VMEM((3, N, 2, 2) + tile, BF),
            pltpu.VMEM((3, N, 2, 2) + tile, BF),
            pltpu.VMEM((2, 2) + tile, F32),
            pltpu.VMEM((4,) + tile, BF),
            pltpu.VMEM((3,) + tile, BF),
            pltpu.VMEM((2,) + tile, BF),
            pltpu.VMEM((3,) + tile, BF),
            pltpu.VMEM((4,) + tile, BF),
            pltpu.VMEM((N, 256, 512), BF),
            pltpu.VMEM((N, 2, 2) + tile, BF),
            DMA((12,)),
        ]
        + twice(14) + twice(6) + twice(3) + twice(3) + twice(12) + twice(4) + twice(4) + twice(3)
        + twice(4) + twice(4) + twice(12) + twice(3) + twice(3) + twice(3) + twice(3) + twice(14),
        compiler_params=pltpu.CompilerParams(
            collective_id=0, has_side_effects=True, vmem_limit_bytes=60 * 2**20
        ),
        name="fused",
    )(
        global_blocks, random_blocks, window_width, queries, key_heads, value_heads, output, output_grad, log_totals
    )


def solution(mesh):
    placed = (
        P(("outer", "inner"), "head"),
        P(("outer", "inner", "head"), None),
        P(("outer", "inner", "head"), None),
        P(("outer", "inner"), "head"),
        P(("outer", "inner"), "head"),
        P("head", ("outer", "inner")),
        P(("outer", "inner"), None),
        P(("outer", "inner")),
        P(),
    )
    return jax.shard_map(
        on_device,
        mesh=mesh,
        in_specs=placed,
        out_specs=(
            P(("outer", "inner"), "head"),
            P(("outer", "inner", "head"), None),
            P(("outer", "inner", "head"), None),
        ),
        check_vma=False,
    )
```

```python
import math

import jax
import jax.numpy as jnp
from jax import lax
from jax.experimental import pallas as pl
from jax.experimental.pallas import tpu as pltpu
from jax.sharding import PartitionSpec as P

MESH = pl.DeviceIdType.MESH
HDIM = 128
BLOCK = 128
N = 4
SCALE = HDIM ** (-0.5)
LOG2E = math.log2(math.e)
ORDER = (0, 1, 3, 2)
UPWARD = (0, 3)
CLOSING = (2, 1, 3, 0)
BACKUP = (2, 3)
YH = [(dy, dh) for dy in range(4) for dh in range(2) if (dy, dh) != (0, 0)]
BF = jnp.bfloat16
F32 = jnp.float32
I32 = jnp.int32
NT = (((1,), (1,)), ((), ()))
TN = (((0,), (0,)), ((), ()))


def place():
    outer = lax.axis_index("outer")
    return outer // N, lax.rem(outer, N), lax.axis_index("inner"), lax.axis_index("head")


def device(z, y, i, h):
    return (z * N + y, i, h)


def shifted(dz=0, dy=0, di=0, dh=0):
    z, y, i, h = place()
    return device(lax.rem(z + dz, N), lax.rem(y + dy, N), lax.rem(i + di, N), lax.rem(h + dh, 2))


def following(shard):
    z, y, i, h = place()
    wrap = (i == N - 1).astype(I32)
    spot = lax.rem(shard + wrap, N)
    cross = wrap * jnp.where(shard == N - 1, 1, 0)
    return device(lax.rem(z + cross, N), y, lax.rem(i + 1, N), h), spot


def preceding(shard):
    z, y, i, h = place()
    wrap = (i == 0).astype(I32)
    spot = lax.rem(shard - wrap + N, N)
    cross = wrap * jnp.where(shard == 0, 1, 0)
    return device(lax.rem(z - cross + N, N), y, lax.rem(i + N - 1, N), h), spot


def greet():
    barrier = pltpu.get_barrier_semaphore()
    found = [shifted(dy=dy, dh=dh) for dy, dh in YH]
    found += [shifted(dz=dz) for dz in range(1, N)]
    found += [shifted(di=di) for di in range(1, N)]
    found += [following(N - 1)[0], preceding(0)[0]]
    for one in found:
        pl.semaphore_signal(barrier, inc=1, device_id=one, device_id_type=MESH)
    return barrier, len(found)


def remote(src, dst, send, recv, to):
    return pltpu.make_async_remote_copy(
        src_ref=src, dst_ref=dst, send_sem=send, recv_sem=recv, device_id=to, device_id_type=MESH
    )


def columns(index, width):
    return pl.ds(pl.multiple_of(index * width, width), width)


def offset_of(k):
    if isinstance(k, int):
        return (0, 1, 3, 2)[k]
    return k + (k == 2).astype(I32) - (k == 3).astype(I32)


def block_slot(block):
    shard = block // 2
    return (shard // (N * N)) * 8 + lax.rem(shard // N, N) * 2 + lax.rem(block, 2)


def fused(
    glob_ref, rand_ref, width_ref, q_ref, k_ref, v_ref, o_ref, g_ref, lse_ref,
    dq, dk, dv,
    og, lseb, sbuf, kvh, intb, intr, ints, stats, qb, gb, kvu, hal, gsend, grecv,
    dqt, acc, dhb, hrn, hrp, ent, rsb, rst, rsr, gacc, dglb, g1r, g2s, g2r, g3r, dqb, outb,
    loc, kvl, kv_s, kv_r, q_s, q_r, st_s, st_r, it_s, it_r, ag_s, ag_r, hn_s, hn_r, hp_s, hp_r, gl_s, gl_r,
    dn_s, dn_r, dp_s, dp_r, rs_s, rs_r, g1_s, g1_r, g2_s, g2_r, g3_s, g3_r, dq_s, dq_r, out_s, out_r,
):
    z, y, i, h = place()
    own_slot = z * 8 + y * 2 + h
    own_col = columns(h * N + y, HDIM)
    loads = [
        pltpu.make_async_copy(o_ref, og.at[0], loc.at[0]),
        pltpu.make_async_copy(g_ref, og.at[1], loc.at[1]),
        pltpu.make_async_copy(lse_ref, lseb, loc.at[2]),
    ]
    keep = [
        pltpu.make_async_copy(k_ref.at[:, own_col], kvu.at[own_slot, 0], loc.at[3]),
        pltpu.make_async_copy(v_ref.at[:, own_col], kvu.at[own_slot, 1], loc.at[4]),
    ]
    stay = [
        pltpu.make_async_copy(q_ref.at[:, columns(y, 512)], qb.at[y], loc.at[5]),
        pltpu.make_async_copy(g_ref.at[:, columns(y, 512)], gb.at[y], loc.at[6]),
    ]
    staged = []
    for n in range(8):
        for side, ref in enumerate((k_ref, v_ref)):
            staged.append(
                pltpu.make_async_copy(ref.at[:, n * HDIM : (n + 1) * HDIM], kvh.at[n, side], kvl.at[2 * n + side])
            )
    for one in staged + keep + loads + stay:
        one.start()
    lane = lax.broadcasted_iota(I32, (8, 128), 1)
    sub = lax.broadcasted_iota(I32, (8, 128), 0)
    row = jnp.zeros((8, 128), I32)
    for b in range(2):
        for r in range(3):
            slot = block_slot(rand_ref[b, r])
            row = jnp.where((lane == b * 3 + r) & (sub == 0), slot, row)
            row = jnp.where((lane == slot) & (sub == 1), b * 3 + r + 1, row)
        row = jnp.where((lane == 6 + b) & (sub == 0), width_ref[b], row)
    intb[...] = row
    barrier, arrivals = greet()
    for one in loads:
        one.wait()
    picker = (
        lax.broadcasted_iota(I32, (8, 512), 1) // HDIM == lax.broadcasted_iota(I32, (8, 512), 0) - 4
    ).astype(BF)
    for c in range(N):
        prod = og[0, :, c * 512 : (c + 1) * 512].astype(F32) * og[1, :, c * 512 : (c + 1) * 512].astype(F32)
        high = prod.astype(BF)
        low = (prod - high.astype(F32)).astype(BF)
        delta = lax.dot_general(picker, high, NT, preferred_element_type=F32)
        delta = delta + lax.dot_general(picker, low, NT, preferred_element_type=F32)
        sbuf[c] = jnp.concatenate([lseb[4 * c : 4 * c + 4, :] * LOG2E, delta[4:8]], axis=0)
    pl.semaphore_wait(barrier, arrivals)

    it_copies = [
        remote(intb, intr.at[y], it_s.at[dy - 1], it_r.at[dy - 1], shifted(dy=dy)) for dy in range(1, N)
    ]
    kv_copies = {}
    for one in staged:
        one.wait()
    for dy, dh in sorted(YH, key=lambda s: ((0, 1, 3, 2)[s[0]], s[1])):
        n = YH.index((dy, dh))
        to = shifted(dy=dy, dh=dh)
        part = lax.rem(h + dh, 2) * N + lax.rem(y + dy, N)
        kv_copies[dy, dh] = remote(kvh.at[part], kvu.at[own_slot], kv_s.at[n], kv_r.at[n], to)
        kv_copies[dy, dh].start()
    for one in it_copies:
        one.start()
    intr[y] = row
    st_copies = [
        remote(sbuf.at[lax.rem(y + dy, N)], stats.at[y], st_s.at[dy - 1], st_r.at[dy - 1], shifted(dy=dy))
        for dy in range(1, N)
    ]
    for one in st_copies:
        one.start()
    own_stats = pltpu.make_async_copy(sbuf.at[y], stats.at[y], loc.at[7])
    own_stats.start()
    q_copies = {}
    for dy in (1, 3, 2):
        c = lax.rem(y + dy, N)
        for side, (ref, dst) in enumerate(((q_ref, qb), (g_ref, gb))):
            n = 2 * (dy - 1) + side
            q_copies[dy, side] = remote(
                ref.at[:, columns(c, 512)], dst.at[y], q_s.at[n], q_r.at[n], shifted(dy=dy)
            )
            q_copies[dy, side].start()

    for one in keep:
        one.wait()

    ag_copies, hn_copies, hp_copies = {}, [], []

    def spread(dy):
        shard = lax.rem(y - dy + N, N)
        for dh in range(2):
            if (dy, dh) != (0, 0):
                kv_copies[dy, dh].wait_recv()
        here = pl.ds(pl.multiple_of(z * 8 + shard * 2, 2), 2)
        for dz in (1, 3):
            n = dy * 3 + dz - 1
            ag_copies[dy, dz] = remote(kvu.at[here], kvu.at[here], ag_s.at[n], ag_r.at[n], shifted(dz=dz))
            ag_copies[dy, dz].start()
        to, spot = following(shard)
        hn_copies.append(remote(kvu.at[here], hal.at[0, spot], hn_s.at[dy], hn_r.at[spot], to))
        hn_copies[-1].start()
        to, spot = preceding(shard)
        hp_copies.append(remote(kvu.at[here], hal.at[1, spot], hp_s.at[dy], hp_r.at[spot], to))
        hp_copies[-1].start()

    def pass_on(dy):
        step = 1 if dy in UPWARD else 3
        ag_copies[dy, step].wait_recv()
        shard = lax.rem(y - dy + N, N)
        here = pl.ds(pl.multiple_of(lax.rem(z - step + N, N) * 8 + shard * 2, 2), 2)
        n = dy * 3 + 1
        ag_copies[dy, 2] = remote(kvu.at[here], kvu.at[here], ag_s.at[n], ag_r.at[n], shifted(dz=step))
        ag_copies[dy, 2].start()

    spread(0)
    spread(1)
    pass_on(0)
    spread(3)
    pass_on(1)
    spread(2)
    pass_on(3)
    pass_on(2)
    for one in it_copies + st_copies:
        one.wait_recv()
    own_stats.wait()
    to_scalar = pltpu.make_async_copy(intr, ints, loc.at[8])
    to_scalar.start()
    to_scalar.wait()
    for shard in range(N):
        ent[shard, 0] = jnp.zeros((2, BLOCK, HDIM), BF)
    for b in range(2):
        dqt[6 + b] = jnp.zeros((HDIM, 512), F32)
    for g in range(2):
        for side in range(2):
            gacc[g, side] = jnp.zeros((BLOCK, HDIM), F32)

    def load_block(shard, b):
        rows = slice(b * BLOCK, (b + 1) * BLOCK)
        query = jnp.concatenate([qb[shard, rows, j * HDIM : (j + 1) * HDIM] for j in range(4)], axis=0)
        grad = jnp.concatenate([gb[shard, rows, j * HDIM : (j + 1) * HDIM] for j in range(4)], axis=0)
        tile = stats[shard, :, rows]
        lse = jnp.concatenate([tile[j : j + 1] for j in range(4)], axis=1)
        delta = jnp.concatenate([tile[4 + j : 5 + j] for j in range(4)], axis=1)
        return query, grad, lse, delta

    def attend(pairs, lses, query, grad, delta):
        count = len(pairs)
        keys = jnp.concatenate([k for k, _ in pairs], axis=0)
        values = jnp.concatenate([v for _, v in pairs], axis=0)
        scores = lax.dot_general(keys, query, NT, preferred_element_type=F32) * (SCALE * LOG2E)
        scores = jnp.concatenate([scores[k * BLOCK : (k + 1) * BLOCK] - lses[k] for k in range(count)], axis=0)
        probs = jnp.exp2(scores)
        prob_grad = lax.dot_general(values, grad, NT, preferred_element_type=F32)
        score_grad = (probs * (prob_grad - delta)).astype(BF)
        value_entry = jnp.dot(probs.astype(BF), grad, preferred_element_type=F32)
        key_entry = jnp.dot(score_grad, query, preferred_element_type=F32)
        turned = lax.dot_general(keys, score_grad, TN, preferred_element_type=F32)
        cut = [slice(k * BLOCK, (k + 1) * BLOCK) for k in range(count)]
        return [key_entry[c] for c in cut], [value_entry[c] for c in cut], turned

    def window(k, add):
        shard = lax.rem(y - offset_of(k) + N, N)
        remote(hal.at[0, shard], hal.at[0, shard], hn_s.at[shard], hn_r.at[shard], shifted(di=1)).wait_recv()
        remote(hal.at[1, shard], hal.at[1, shard], hp_s.at[shard], hp_r.at[shard], shifted(di=1)).wait_recv()
        for b in range(2):
            query, grad, lse, delta = load_block(shard, b)
            width = ints[shard, 0, 6 + b]
            block_id = ((z * N + shard) * N + i) * 2 + b
            total = None
            for group in ((0, 1), (2, 3), (4,)):
                pairs, lses = [], []
                for e in group:
                    at = b + e - 2
                    if at < 0:
                        pairs.append((hal[0, shard, at + 2, 0], hal[0, shard, at + 2, 1]))
                    elif at >= 2:
                        pairs.append((hal[1, shard, at - 2, 0], hal[1, shard, at - 2, 1]))
                    else:
                        slot = z * 8 + shard * 2 + at
                        pairs.append((kvu[slot, 0], kvu[slot, 1]))
                    target = block_id + e - 2
                    ok = (abs(e - 2) <= width) & (target >= 0) & (target < 128)
                    lses.append(lse + jnp.where(ok, 0.0, 1e6).astype(F32))
                dks, dvs, turned = attend(pairs, lses, query, grad, delta)
                total = turned if total is None else total + turned
                for e, dk_e, dv_e in zip(group, dks, dvs):
                    at = b + e
                    if b == 0 or at == 5:
                        acc[shard, at, 0] = dk_e
                        acc[shard, at, 1] = dv_e
                    else:
                        acc[shard, at, 0] += dk_e
                        acc[shard, at, 1] += dv_e
            if add:
                dqt[2 * k + b] += total
            else:
                dqt[2 * k + b] = total
        for n, start in enumerate((0, 4)):
            for b in range(2):
                dhb[n, shard, b, 0] = (acc[shard, start + b, 0] * SCALE).astype(BF)
                dhb[n, shard, b, 1] = acc[shard, start + b, 1].astype(BF)
        to, spot = preceding(shard)
        remote(dhb.at[0, shard], hrn.at[spot], dn_s.at[shard], dn_r.at[spot], to).start()
        to, spot = following(shard)
        remote(dhb.at[1, shard], hrp.at[spot], dp_s.at[shard], dp_r.at[spot], to).start()

    def wait_queries(k):
        dy = offset_of(k)
        for side, (ref, dst) in enumerate(((q_ref, qb), (g_ref, gb))):
            n = 2 * (dy - 1) + side
            remote(
                ref.at[:, columns(y, 512)], dst.at[y], q_s.at[n], q_r.at[n], shifted(dy=1)
            ).wait_recv()

    for one in stay:
        one.wait()
    def early(k, carry):
        @pl.when(k > 0)
        def _():
            wait_queries(k)

        window(k, False)
        return carry

    lax.fori_loop(0, 1, early, 0)
    lax.fori_loop(1, 3, early, 0)

    for dy in range(N):
        for dz in range(1, N):
            if dz == 2 or dz == (3 if dy in UPWARD else 1):
                ag_copies[dy, dz].wait_recv()
    for g in range(2):
        gsend[g] = kvu[block_slot(glob_ref[g])]
    gl_copies = [
        remote(gsend, grecv.at[di], gl_s.at[di - 1], gl_r.at[di - 1], shifted(di=di)) for di in range(1, N)
    ]
    for one in gl_copies:
        one.start()
    grecv[0] = gsend[...]

    def random(k, carry):
        @pl.when(k == 3)
        def _():
            wait_queries(k)

        shard = lax.rem(y - offset_of(k) + N, N)
        for b in range(2):
            query, grad, lse, delta = load_block(shard, b)
            total = None
            for group in ((0, 1), (2,)):
                slots = [ints[shard, 0, b * 3 + r] for r in group]
                pairs = [(kvu[s, 0], kvu[s, 1]) for s in slots]
                dks, dvs, turned = attend(pairs, [lse] * len(group), query, grad, delta)
                total = turned if total is None else total + turned
                for r, dk_e, dv_e in zip(group, dks, dvs):
                    ent[shard, 1 + b * 3 + r, 0] = (dk_e * SCALE).astype(BF)
                    ent[shard, 1 + b * 3 + r, 1] = dv_e.astype(BF)
            dqt[2 * k + b] += total
        return carry

    lax.fori_loop(0, N, random, 0)

    def named(slot):
        total = None
        for shard in range(N):
            one = ent[shard, ints[shard, 1, slot]].astype(F32)
            total = one if total is None else total + one
        return total

    rs_copies = {}

    def fill(dz, dy):
        shard = lax.rem(y + dy, N)
        to = lax.rem(z + dz, N)

        def put(b, carry):
            rsb[dz - 1, dy, b] = named(to * 8 + shard * 2 + b).astype(BF)
            return carry

        lax.fori_loop(0, 2, put, 0)

    def rs_send(dz, dy, dst, to):
        n = dy * 3 + dz - 1
        rs_copies[dz, dy] = remote(rsb.at[dz - 1, dy], dst, rs_s.at[n], rs_r.at[n], to)
        rs_copies[dz, dy].start()

    def rs_first(dys):
        for dy in dys:
            fill(2, dy)
            rs_send(2, dy, rst.at[dy], shifted(dz=1 if dy in BACKUP else 3))
        for dy in dys:
            dz = 3 if dy in BACKUP else 1
            fill(dz, dy)
            rs_send(dz, dy, rsr.at[dz // 2, dy], shifted(dz=dz))
        for dy in dys:
            fill(1 if dy in BACKUP else 3, dy)

    def rs_second(dys):
        for dy in dys:
            dz = 1 if dy in BACKUP else 3
            rs_copies[2, dy].wait_recv()

            def join(b, carry, dz=dz, dy=dy):
                rsb[dz - 1, dy, b] = (rsb[dz - 1, dy, b].astype(F32) + rst[dy, b].astype(F32)).astype(BF)
                return carry

            lax.fori_loop(0, 2, join, 0)
            rs_send(dz, dy, rsr.at[dz // 2, dy], shifted(dz=dz))

    rs_first(CLOSING[:2])

    for one in gl_copies:
        one.wait_recv()
    globe = []
    for g in range(2):
        source = lax.rem(i - lax.rem(glob_ref[g] // 2, N) + N, N)
        globe.append(source)

    def dq_copy(k):
        dy = offset_of(k)
        shard = lax.rem(y - dy + N, N)
        return remote(
            dqb.at[shard], dq.at[:, columns(y, 512)], dq_s.at[dy - 1], dq_r.at[dy - 1], device(z, shard, i, h)
        )

    dq_home = pltpu.make_async_copy(dqb.at[y], dq.at[:, columns(y, 512)], loc.at[9])

    def whole(k, carry):
        shard = lax.rem(y - offset_of(k) + N, N)
        for b in range(2):
            query, grad, lse, delta = load_block(shard, b)
            pairs = [(grecv[globe[g], g, 0], grecv[globe[g], g, 1]) for g in range(2)]
            dks, dvs, turned = attend(pairs, [lse] * 2, query, grad, delta)
            for g in range(2):
                gacc[g, 0] += dks[g]
                gacc[g, 1] += dvs[g]
            done = (jnp.transpose(dqt[2 * k + b] + turned) * SCALE).astype(BF)
            for j in range(4):
                dqb[shard, b * BLOCK : (b + 1) * BLOCK, j * HDIM : (j + 1) * HDIM] = done[
                    j * BLOCK : (j + 1) * BLOCK
                ]

        @pl.when(k == 0)
        def _():
            dq_home.start()

        @pl.when(k > 0)
        def _():
            dq_copy(k).start()

        return carry

    def late(k, carry):
        window(k, True)
        return carry

    lax.fori_loop(0, 3, whole, 0)
    rs_second(CLOSING[:2])
    lax.fori_loop(3, 4, late, 0)
    lax.fori_loop(3, 4, whole, 0)

    for g in range(2):
        dglb[2 * g] = (gacc[g, 0] * SCALE).astype(BF)
        dglb[2 * g + 1] = gacc[g, 1].astype(BF)
    g1_copies = [
        remote(dglb.at[lax.rem(i + di, N)], g1r.at[di - 1], g1_s.at[di - 1], g1_r.at[di - 1], shifted(di=di))
        for di in range(1, N)
    ]
    for one in g1_copies:
        one.start()
    for one in g1_copies:
        one.wait_recv()
    partial = dglb[i].astype(F32)
    for n in range(3):
        partial = partial + g1r[n].astype(F32)
    g2s[0] = partial.astype(BF)
    g2_copies = [
        remote(g2s.at[0], g2r.at[dz - 1], g2_s.at[dz - 1], g2_r.at[dz - 1], shifted(dz=dz)) for dz in range(1, N)
    ]
    for one in g2_copies:
        one.start()
    rs_first(CLOSING[2:])
    for one in g2_copies:
        one.wait_recv()
    for n in range(3):
        partial = partial + g2r[n].astype(F32)
    g2s[1] = partial.astype(BF)
    g3r[i] = g2s[1]
    g3_copies = [
        remote(g2s.at[1], g3r.at[i], g3_s.at[di - 1], g3_r.at[di - 1], shifted(di=di)) for di in range(1, N)
    ]
    for one in g3_copies:
        one.start()
    rs_second(CLOSING[2:])
    for one in g3_copies:
        one.wait_recv()
    for shard in range(N):
        remote(dhb.at[0, shard], hrn.at[shard], dn_s.at[shard], dn_r.at[shard], shifted(di=1)).wait_recv()
        remote(dhb.at[1, shard], hrp.at[shard], dp_s.at[shard], dp_r.at[shard], shifted(di=1)).wait_recv()

    out_copies, home = [], []
    for dy in CLOSING:
        shard = lax.rem(y + dy, N)
        rs_copies[1, dy].wait_recv()
        rs_copies[3, dy].wait_recv()

        def close(b, carry, shard=shard, dy=dy):
            block_id = ((z * N + shard) * N + i) * 2 + b
            extra = named(z * 8 + shard * 2 + b)
            for side in range(2):
                total = acc[shard, 2 + b, side] * (SCALE if side == 0 else 1.0) + extra[side]
                total = total + hrn[shard, b, side].astype(F32) + hrp[shard, b, side].astype(F32)
                for n in range(2):
                    total = total + rsr[n, dy, b, side].astype(F32)
                for g in range(2):
                    hit = (jnp.zeros((BLOCK, HDIM), I32) + glob_ref[g]) == block_id
                    total = total + jnp.where(hit, g3r[2 * g + side].astype(F32), 0.0)
                outb[shard, b, side] = total.astype(BF)
            return carry

        lax.fori_loop(0, 2, close, 0)
        for dh in range(2):
            b = lax.rem(h + dh, 2)
            for side, ref in enumerate((dk, dv)):
                if (dy, dh) == (0, 0):
                    home.append(
                        pltpu.make_async_copy(outb.at[shard, b, side], ref.at[:, own_col], loc.at[10 + side])
                    )
                    home[-1].start()
                else:
                    n = 2 * YH.index((dy, dh)) + side
                    out_copies.append(
                        remote(
                            outb.at[shard, b, side],
                            ref.at[:, own_col],
                            out_s.at[n],
                            out_r.at[n],
                            shifted(dy=dy, dh=dh),
                        )
                    )
                    out_copies[-1].start()
    for one in out_copies + home + [dq_home]:
        one.wait()
    for k in range(1, N):
        dq_copy(k).wait()
    for one in list(kv_copies.values()) + list(q_copies.values()) + it_copies + st_copies:
        one.wait_send()
    for one in list(ag_copies.values()) + list(rs_copies.values()):
        one.wait_send()
    for one in hn_copies + hp_copies + gl_copies + g1_copies + g2_copies + g3_copies:
        one.wait_send()
    for shard in range(N):
        remote(dhb.at[0, shard], hrn.at[shard], dn_s.at[shard], dn_r.at[shard], shifted(di=1)).wait_send()
        remote(dhb.at[1, shard], hrp.at[shard], dp_s.at[shard], dp_r.at[shard], shifted(di=1)).wait_send()


def hand_over(a, b, c, a_out, b_out, c_out, wide, tall, sems_in, sems_out):
    moves = [(a.at[pl.ds(64 * n, 64)], wide.at[n], a_out.at[pl.ds(64 * n, 64)]) for n in range(4)]
    moves += [(b, tall.at[0], b_out), (c, tall.at[1], c_out)]
    come = [pltpu.make_async_copy(src, via, sems_in.at[n]) for n, (src, via, _) in enumerate(moves)]
    leave = [pltpu.make_async_copy(via, dst, sems_out.at[n]) for n, (_, via, dst) in enumerate(moves)]
    for one in come:
        one.start()
    for first, then in zip(come, leave):
        first.wait()
        then.start()
    for one in leave:
        one.wait()


HBM = pl.BlockSpec(memory_space=pltpu.HBM)
SMEM = pl.BlockSpec(memory_space=pltpu.SMEM)
DMA = pltpu.SemaphoreType.DMA


def on_device(
    queries, key_heads, value_heads, output, output_grad, log_totals, random_blocks, window_width, global_blocks
):
    shape = jax.ShapeDtypeStruct
    tile = (BLOCK, HDIM)
    twice = lambda n: [DMA((n,)), DMA((n,))]
    results = pl.pallas_call(
        fused,
        out_shape=(
            shape((256, 2048), BF),
            shape((BLOCK, 1024), BF),
            shape((BLOCK, 1024), BF),
        ),
        in_specs=[SMEM, SMEM, SMEM] + [HBM] * 6,
        out_specs=(HBM, HBM, HBM),
        scratch_shapes=[
            pltpu.VMEM((2, 256, 2048), BF),
            pltpu.VMEM((16, 256), F32),
            pltpu.VMEM((N, 8, 256), F32),
            pltpu.VMEM((8, 2) + tile, BF),
            pltpu.VMEM((8, 128), I32),
            pltpu.VMEM((N, 8, 128), I32),
            pltpu.SMEM((N, 8, 128), I32),
            pltpu.VMEM((N, 8, 256), F32),
            pltpu.VMEM((N, 256, 512), BF),
            pltpu.VMEM((N, 256, 512), BF),
            pltpu.VMEM((32, 2) + tile, BF),
            pltpu.VMEM((2, N, 2, 2) + tile, BF),
            pltpu.VMEM((2, 2) + tile, BF),
            pltpu.VMEM((N, 2, 2) + tile, BF),
            pltpu.VMEM((8, HDIM, 512), F32),
            pltpu.VMEM((N, 6, 2) + tile, F32),
            pltpu.VMEM((2, N, 2, 2) + tile, BF),
            pltpu.VMEM((N, 2, 2) + tile, BF),
            pltpu.VMEM((N, 2, 2) + tile, BF),
            pltpu.VMEM((N, 7, 2) + tile, BF),
            pltpu.VMEM((3, N, 2, 2) + tile, BF),
            pltpu.VMEM((N, 2, 2) + tile, BF),
            pltpu.VMEM((2, N, 2, 2) + tile, BF),
            pltpu.VMEM((2, 2) + tile, F32),
            pltpu.VMEM((4,) + tile, BF),
            pltpu.VMEM((3,) + tile, BF),
            pltpu.VMEM((2,) + tile, BF),
            pltpu.VMEM((3,) + tile, BF),
            pltpu.VMEM((4,) + tile, BF),
            pltpu.VMEM((N, 256, 512), BF),
            pltpu.VMEM((N, 2, 2) + tile, BF),
            DMA((12,)),
            DMA((16,)),
        ]
        + twice(7) + twice(6) + twice(3) + twice(3) + twice(12) + twice(4) + twice(4) + twice(3)
        + twice(4) + twice(4) + twice(12) + twice(3) + twice(3) + twice(3) + twice(3) + twice(14),
        compiler_params=pltpu.CompilerParams(
            collective_id=0, has_side_effects=True, vmem_limit_bytes=60 * 2**20
        ),
        name="fused",
    )(
        global_blocks, random_blocks, window_width, queries, key_heads, value_heads, output, output_grad, log_totals
    )
    return pl.pallas_call(
        hand_over,
        out_shape=tuple(shape(one.shape, BF) for one in results),
        in_specs=[HBM] * 3,
        out_specs=(HBM, HBM, HBM),
        scratch_shapes=[
            pltpu.VMEM((4, 64, 2048), BF),
            pltpu.VMEM((2, BLOCK, 1024), BF),
            DMA((6,)),
            DMA((6,)),
        ],
        compiler_params=pltpu.CompilerParams(vmem_limit_bytes=60 * 2**20),
        name="hand_over",
    )(*results)


def solution(mesh):
    placed = (
        P(("outer", "inner"), "head"),
        P(("outer", "inner", "head"), None),
        P(("outer", "inner", "head"), None),
        P(("outer", "inner"), "head"),
        P(("outer", "inner"), "head"),
        P("head", ("outer", "inner")),
        P(("outer", "inner"), None),
        P(("outer", "inner")),
        P(),
    )
    return jax.shard_map(
        on_device,
        mesh=mesh,
        in_specs=placed,
        out_specs=(
            P(("outer", "inner"), "head"),
            P(("outer", "inner", "head"), None),
            P(("outer", "inner", "head"), None),
        ),
        check_vma=False,
    )
```

```python
import math

import jax
import jax.numpy as jnp
from jax import lax
from jax.experimental import pallas as pl
from jax.experimental.pallas import tpu as pltpu
from jax.sharding import PartitionSpec as P

MESH = pl.DeviceIdType.MESH
HDIM = 128
BLOCK = 128
N = 4
SCALE = HDIM ** (-0.5)
LOG2E = math.log2(math.e)
ORDER = (0, 1, 3, 2)
UPWARD = (0, 3)
WINDOW_GROUPS = ((0, 1), (2, 3), (4,))
RANDOM_GROUPS = ((0, 1), (2,))
CLOSING = (2, 1, 3, 0)
BACKUP = (2, 3)
YH = [(dy, dh) for dy in range(4) for dh in range(2) if (dy, dh) != (0, 0)]
BF = jnp.bfloat16
F32 = jnp.float32
I32 = jnp.int32
NT = (((1,), (1,)), ((), ()))
TN = (((0,), (0,)), ((), ()))


def place():
    outer = lax.axis_index("outer")
    return outer // N, lax.rem(outer, N), lax.axis_index("inner"), lax.axis_index("head")


def device(z, y, i, h):
    return (z * N + y, i, h)


def shifted(dz=0, dy=0, di=0, dh=0):
    z, y, i, h = place()
    return device(lax.rem(z + dz, N), lax.rem(y + dy, N), lax.rem(i + di, N), lax.rem(h + dh, 2))


def following(shard):
    z, y, i, h = place()
    wrap = (i == N - 1).astype(I32)
    spot = lax.rem(shard + wrap, N)
    cross = wrap * jnp.where(shard == N - 1, 1, 0)
    return device(lax.rem(z + cross, N), y, lax.rem(i + 1, N), h), spot


def preceding(shard):
    z, y, i, h = place()
    wrap = (i == 0).astype(I32)
    spot = lax.rem(shard - wrap + N, N)
    cross = wrap * jnp.where(shard == 0, 1, 0)
    return device(lax.rem(z - cross + N, N), y, lax.rem(i + N - 1, N), h), spot


def greet():
    barrier = pltpu.get_barrier_semaphore()
    found = [shifted(dy=dy, dh=dh) for dy, dh in YH]
    found += [shifted(dz=dz) for dz in range(1, N)]
    found += [shifted(di=di) for di in range(1, N)]
    found += [following(N - 1)[0], preceding(0)[0]]
    for one in found:
        pl.semaphore_signal(barrier, inc=1, device_id=one, device_id_type=MESH)
    return barrier, len(found)


def remote(src, dst, send, recv, to):
    return pltpu.make_async_remote_copy(
        src_ref=src, dst_ref=dst, send_sem=send, recv_sem=recv, device_id=to, device_id_type=MESH
    )


def columns(index, width):
    return pl.ds(pl.multiple_of(index * width, width), width)


def offset_of(k):
    if isinstance(k, int):
        return (0, 1, 3, 2)[k]
    return k + (k == 2).astype(I32) - (k == 3).astype(I32)


def block_slot(block):
    shard = block // 2
    return (shard // (N * N)) * 8 + lax.rem(shard // N, N) * 2 + lax.rem(block, 2)


def fused(
    glob_ref, rand_ref, width_ref, q_ref, k_ref, v_ref, o_ref, g_ref, lse_ref,
    dq, dkv,
    og, lseb, sbuf, kvh, intb, intr, ints, stats, qb, gb, kvu, hal, gsend, grecv,
    dqt, acc, dhb, hrn, hrp, ent, rsb, rst, rsr, gacc, dglb, g1r, g2s, g2r, g3r, dqb, outb,
    loc, kvl, kv_s, kv_r, q_s, q_r, st_s, st_r, it_s, it_r, ag_s, ag_r, hn_s, hn_r, hp_s, hp_r, gl_s, gl_r,
    dn_s, dn_r, dp_s, dp_r, rs_s, rs_r, g1_s, g1_r, g2_s, g2_r, g3_s, g3_r, dq_s, dq_r, out_s, out_r,
):
    z, y, i, h = place()
    own_slot = z * 8 + y * 2 + h
    own_col = columns(h * N + y, HDIM)
    loads = [
        pltpu.make_async_copy(o_ref, og.at[0], loc.at[0]),
        pltpu.make_async_copy(g_ref, og.at[1], loc.at[1]),
        pltpu.make_async_copy(lse_ref, lseb, loc.at[2]),
    ]
    keep = [
        pltpu.make_async_copy(k_ref.at[:, own_col], kvu.at[own_slot, 0], loc.at[3]),
        pltpu.make_async_copy(v_ref.at[:, own_col], kvu.at[own_slot, 1], loc.at[4]),
    ]
    stay = [
        pltpu.make_async_copy(q_ref.at[:, columns(y, 512)], qb.at[y], loc.at[5]),
        pltpu.make_async_copy(g_ref.at[:, columns(y, 512)], gb.at[y], loc.at[6]),
    ]
    staged = []
    for n in range(8):
        for side, ref in enumerate((k_ref, v_ref)):
            staged.append(
                pltpu.make_async_copy(ref.at[:, n * HDIM : (n + 1) * HDIM], kvh.at[n, side], kvl.at[2 * n + side])
            )
    for one in staged + keep + loads + stay:
        one.start()
    lane = lax.broadcasted_iota(I32, (8, 128), 1)
    sub = lax.broadcasted_iota(I32, (8, 128), 0)
    row = jnp.zeros((8, 128), I32)
    for b in range(2):
        for r in range(3):
            slot = block_slot(rand_ref[b, r])
            row = jnp.where((lane == b * 3 + r) & (sub == 0), slot, row)
            row = jnp.where((lane == slot) & (sub == 1), b * 3 + r + 1, row)
        row = jnp.where((lane == 6 + b) & (sub == 0), width_ref[b], row)
    intb[...] = row
    barrier, arrivals = greet()
    pl.semaphore_wait(barrier, arrivals)

    it_copies = [
        remote(intb, intr.at[y], it_s.at[dy - 1], it_r.at[dy - 1], shifted(dy=dy)) for dy in range(1, N)
    ]
    kv_copies = {}
    for one in staged:
        one.wait()
    for dy, dh in sorted(YH, key=lambda s: ((0, 1, 3, 2)[s[0]], s[1])):
        n = YH.index((dy, dh))
        to = shifted(dy=dy, dh=dh)
        part = lax.rem(h + dh, 2) * N + lax.rem(y + dy, N)
        kv_copies[dy, dh] = remote(kvh.at[part], kvu.at[own_slot], kv_s.at[n], kv_r.at[n], to)
        kv_copies[dy, dh].start()
    for one in it_copies:
        one.start()
    intr[y] = row
    for one in loads:
        one.wait()
    picker = (
        lax.broadcasted_iota(I32, (8, 512), 1) // HDIM == lax.broadcasted_iota(I32, (8, 512), 0) - 4
    ).astype(BF)
    for c in range(N):
        prod = og[0, :, c * 512 : (c + 1) * 512].astype(F32) * og[1, :, c * 512 : (c + 1) * 512].astype(F32)
        high = prod.astype(BF)
        low = (prod - high.astype(F32)).astype(BF)
        delta = lax.dot_general(picker, high, NT, preferred_element_type=F32)
        delta = delta + lax.dot_general(picker, low, NT, preferred_element_type=F32)
        sbuf[c] = jnp.concatenate([lseb[4 * c : 4 * c + 4, :] * LOG2E, delta[4:8]], axis=0)
    st_copies = [
        remote(sbuf.at[lax.rem(y + dy, N)], stats.at[y], st_s.at[dy - 1], st_r.at[dy - 1], shifted(dy=dy))
        for dy in range(1, N)
    ]
    for one in st_copies:
        one.start()
    own_stats = pltpu.make_async_copy(sbuf.at[y], stats.at[y], loc.at[7])
    own_stats.start()
    q_copies = {}

    def ask(dy):
        c = lax.rem(y + dy, N)
        for side, (ref, dst) in enumerate(((q_ref, qb), (g_ref, gb))):
            n = 2 * (dy - 1) + side
            q_copies[dy, side] = remote(
                ref.at[:, columns(c, 512)], dst.at[y], q_s.at[n], q_r.at[n], shifted(dy=dy)
            )
            q_copies[dy, side].start()

    ask(1)
    for one in keep:
        one.wait()

    ag_copies, hn_copies, hp_copies = {}, [], []

    def spread(dy):
        shard = lax.rem(y - dy + N, N)
        for dh in range(2):
            if (dy, dh) != (0, 0):
                kv_copies[dy, dh].wait_recv()
        here = pl.ds(pl.multiple_of(z * 8 + shard * 2, 2), 2)
        for dz in (1, 3):
            n = dy * 3 + dz - 1
            ag_copies[dy, dz] = remote(kvu.at[here], kvu.at[here], ag_s.at[n], ag_r.at[n], shifted(dz=dz))
            ag_copies[dy, dz].start()
        to, spot = following(shard)
        hn_copies.append(remote(kvu.at[here], hal.at[0, spot], hn_s.at[dy], hn_r.at[spot], to))
        hn_copies[-1].start()
        to, spot = preceding(shard)
        hp_copies.append(remote(kvu.at[here], hal.at[1, spot], hp_s.at[dy], hp_r.at[spot], to))
        hp_copies[-1].start()

    def pass_on(dy):
        step = 1 if dy in UPWARD else 3
        ag_copies[dy, step].wait_recv()
        shard = lax.rem(y - dy + N, N)
        here = pl.ds(pl.multiple_of(lax.rem(z - step + N, N) * 8 + shard * 2, 2), 2)
        n = dy * 3 + 1
        ag_copies[dy, 2] = remote(kvu.at[here], kvu.at[here], ag_s.at[n], ag_r.at[n], shifted(dz=step))
        ag_copies[dy, 2].start()

    spread(0)
    ask(3)
    spread(1)
    pass_on(0)
    spread(3)
    pass_on(1)
    spread(2)
    for one in it_copies + st_copies:
        one.wait_recv()
    own_stats.wait()
    to_scalar = pltpu.make_async_copy(intr, ints, loc.at[8])
    to_scalar.start()
    to_scalar.wait()
    for shard in range(N):
        ent[shard, 0] = jnp.zeros((2, BLOCK, HDIM), BF)
    for b in range(2):
        dqt[6 + b] = jnp.zeros((HDIM, 512), F32)
    for g in range(2):
        for side in range(2):
            gacc[g, side] = jnp.zeros((BLOCK, HDIM), F32)

    def load_block(shard, b):
        rows = slice(b * BLOCK, (b + 1) * BLOCK)
        query = jnp.concatenate([qb[shard, rows, j * HDIM : (j + 1) * HDIM] for j in range(4)], axis=0)
        grad = jnp.concatenate([gb[shard, rows, j * HDIM : (j + 1) * HDIM] for j in range(4)], axis=0)
        tile = stats[shard, :, rows]
        lse = jnp.concatenate([tile[j : j + 1] for j in range(4)], axis=1)
        delta = jnp.concatenate([tile[4 + j : 5 + j] for j in range(4)], axis=1)
        return query, grad, lse, delta

    def attend(pairs, lses, query, grad, delta):
        count = len(pairs)
        keys = jnp.concatenate([k for k, _ in pairs], axis=0)
        values = jnp.concatenate([v for _, v in pairs], axis=0)
        scores = lax.dot_general(keys, query, NT, preferred_element_type=F32) * (SCALE * LOG2E)
        scores = jnp.concatenate([scores[k * BLOCK : (k + 1) * BLOCK] - lses[k] for k in range(count)], axis=0)
        probs = jnp.exp2(scores)
        prob_grad = lax.dot_general(values, grad, NT, preferred_element_type=F32)
        score_grad = (probs * (prob_grad - delta)).astype(BF)
        value_entry = jnp.dot(probs.astype(BF), grad, preferred_element_type=F32)
        key_entry = jnp.dot(score_grad, query, preferred_element_type=F32)
        turned = lax.dot_general(keys, score_grad, TN, preferred_element_type=F32)
        cut = [slice(k * BLOCK, (k + 1) * BLOCK) for k in range(count)]
        return [key_entry[c] for c in cut], [value_entry[c] for c in cut], turned

    def window(k, add):
        shard = lax.rem(y - offset_of(k) + N, N)
        remote(hal.at[0, shard], hal.at[0, shard], hn_s.at[shard], hn_r.at[shard], shifted(di=1)).wait_recv()
        remote(hal.at[1, shard], hal.at[1, shard], hp_s.at[shard], hp_r.at[shard], shifted(di=1)).wait_recv()
        for b in range(2):
            query, grad, lse, delta = load_block(shard, b)
            width = ints[shard, 0, 6 + b]
            block_id = ((z * N + shard) * N + i) * 2 + b
            total = None
            for group in WINDOW_GROUPS:
                pairs, lses = [], []
                for e in group:
                    at = b + e - 2
                    if at < 0:
                        pairs.append((hal[0, shard, at + 2, 0], hal[0, shard, at + 2, 1]))
                    elif at >= 2:
                        pairs.append((hal[1, shard, at - 2, 0], hal[1, shard, at - 2, 1]))
                    else:
                        slot = z * 8 + shard * 2 + at
                        pairs.append((kvu[slot, 0], kvu[slot, 1]))
                    target = block_id + e - 2
                    ok = (abs(e - 2) <= width) & (target >= 0) & (target < 128)
                    lses.append(lse + jnp.where(ok, 0.0, 1e6).astype(F32))
                dks, dvs, turned = attend(pairs, lses, query, grad, delta)
                total = turned if total is None else total + turned
                for e, dk_e, dv_e in zip(group, dks, dvs):
                    at = b + e
                    if b == 0 or at == 5:
                        acc[shard, at, 0] = dk_e
                        acc[shard, at, 1] = dv_e
                    else:
                        acc[shard, at, 0] += dk_e
                        acc[shard, at, 1] += dv_e
            if add:
                dqt[2 * k + b] += total
            else:
                dqt[2 * k + b] = total
        for n, start in enumerate((0, 4)):
            for b in range(2):
                dhb[n, shard, b, 0] = (acc[shard, start + b, 0] * SCALE).astype(BF)
                dhb[n, shard, b, 1] = acc[shard, start + b, 1].astype(BF)
        to, spot = preceding(shard)
        remote(dhb.at[0, shard], hrn.at[spot], dn_s.at[shard], dn_r.at[spot], to).start()
        to, spot = following(shard)
        remote(dhb.at[1, shard], hrp.at[spot], dp_s.at[shard], dp_r.at[spot], to).start()

    def wait_queries(k):
        dy = offset_of(k)
        for side, (ref, dst) in enumerate(((q_ref, qb), (g_ref, gb))):
            n = 2 * (dy - 1) + side
            remote(
                ref.at[:, columns(y, 512)], dst.at[y], q_s.at[n], q_r.at[n], shifted(dy=1)
            ).wait_recv()

    for one in stay:
        one.wait()
    def early(k, carry):
        @pl.when(k > 0)
        def _():
            wait_queries(k)

        window(k, False)
        return carry

    lax.fori_loop(0, 1, early, 0)
    ask(2)
    pass_on(3)
    pass_on(2)
    lax.fori_loop(1, 3, early, 0)

    for dy in range(N):
        for dz in range(1, N):
            if dz == 2 or dz == (3 if dy in UPWARD else 1):
                ag_copies[dy, dz].wait_recv()
    for g in range(2):
        gsend[g] = kvu[block_slot(glob_ref[g])]
    gl_copies = [
        remote(gsend, grecv.at[di], gl_s.at[di - 1], gl_r.at[di - 1], shifted(di=di)) for di in range(1, N)
    ]
    for one in gl_copies:
        one.start()
    grecv[0] = gsend[...]

    def random(k, carry):
        @pl.when(k == 3)
        def _():
            wait_queries(k)

        shard = lax.rem(y - offset_of(k) + N, N)
        for b in range(2):
            query, grad, lse, delta = load_block(shard, b)
            total = None
            for group in RANDOM_GROUPS:
                slots = [ints[shard, 0, b * 3 + r] for r in group]
                pairs = [(kvu[s, 0], kvu[s, 1]) for s in slots]
                dks, dvs, turned = attend(pairs, [lse] * len(group), query, grad, delta)
                total = turned if total is None else total + turned
                for r, dk_e, dv_e in zip(group, dks, dvs):
                    ent[shard, 1 + b * 3 + r, 0] = (dk_e * SCALE).astype(BF)
                    ent[shard, 1 + b * 3 + r, 1] = dv_e.astype(BF)
            dqt[2 * k + b] += total
        return carry

    lax.fori_loop(0, N, random, 0)

    def named(slot):
        total = None
        for shard in range(N):
            one = ent[shard, ints[shard, 1, slot]].astype(F32)
            total = one if total is None else total + one
        return total

    rs_copies = {}

    def fill(dz, dy):
        shard = lax.rem(y + dy, N)
        to = lax.rem(z + dz, N)

        def put(b, carry):
            rsb[dz - 1, dy, b] = named(to * 8 + shard * 2 + b).astype(BF)
            return carry

        lax.fori_loop(0, 2, put, 0)

    def rs_send(dz, dy, dst, to):
        n = dy * 3 + dz - 1
        rs_copies[dz, dy] = remote(rsb.at[dz - 1, dy], dst, rs_s.at[n], rs_r.at[n], to)
        rs_copies[dz, dy].start()

    def rs_fill(dys):
        for dy in dys:
            fill(2, dy)
        for dy in dys:
            fill(3 if dy in BACKUP else 1, dy)
        for dy in dys:
            fill(1 if dy in BACKUP else 3, dy)

    def rs_first(dys):
        for dy in dys:
            rs_send(2, dy, rst.at[dy], shifted(dz=1 if dy in BACKUP else 3))
        for dy in dys:
            dz = 3 if dy in BACKUP else 1
            rs_send(dz, dy, rsr.at[dz // 2, dy], shifted(dz=dz))

    def rs_second(dys):
        for dy in dys:
            dz = 1 if dy in BACKUP else 3
            rs_copies[2, dy].wait_recv()

            def join(b, carry, dz=dz, dy=dy):
                rsb[dz - 1, dy, b] = (rsb[dz - 1, dy, b].astype(F32) + rst[dy, b].astype(F32)).astype(BF)
                return carry

            lax.fori_loop(0, 2, join, 0)
            rs_send(dz, dy, rsr.at[dz // 2, dy], shifted(dz=dz))

    rs_fill(CLOSING[:2])
    rs_first(CLOSING[:2])

    for one in gl_copies:
        one.wait_recv()
    globe = []
    for g in range(2):
        source = lax.rem(i - lax.rem(glob_ref[g] // 2, N) + N, N)
        globe.append(source)

    def dq_copy(k):
        dy = offset_of(k)
        shard = lax.rem(y - dy + N, N)
        return remote(
            dqb.at[shard], dq.at[:, columns(y, 512)], dq_s.at[dy - 1], dq_r.at[dy - 1], device(z, shard, i, h)
        )

    dq_home = pltpu.make_async_copy(dqb.at[y], dq.at[:, columns(y, 512)], loc.at[9])

    def whole(k, carry):
        shard = lax.rem(y - offset_of(k) + N, N)
        for b in range(2):
            query, grad, lse, delta = load_block(shard, b)
            pairs = [(grecv[globe[g], g, 0], grecv[globe[g], g, 1]) for g in range(2)]
            dks, dvs, turned = attend(pairs, [lse] * 2, query, grad, delta)
            for g in range(2):
                gacc[g, 0] += dks[g]
                gacc[g, 1] += dvs[g]
            dqt[2 * k + b] += turned
        return carry

    def give_query(k, carry):
        shard = lax.rem(y - offset_of(k) + N, N)
        for b in range(2):
            done = (jnp.transpose(dqt[2 * k + b]) * SCALE).astype(BF)
            for j in range(4):
                dqb[shard, b * BLOCK : (b + 1) * BLOCK, j * HDIM : (j + 1) * HDIM] = done[
                    j * BLOCK : (j + 1) * BLOCK
                ]

        @pl.when(k == 0)
        def _():
            dq_home.start()

        @pl.when(k > 0)
        def _():
            dq_copy(k).start()

        return carry

    def late(k, carry):
        window(k, True)
        return carry

    lax.fori_loop(0, N, whole, 0)
    for g in range(2):
        dglb[2 * g] = (gacc[g, 0] * SCALE).astype(BF)
        dglb[2 * g + 1] = gacc[g, 1].astype(BF)
    g1_copies = [
        remote(dglb.at[lax.rem(i + di, N)], g1r.at[di - 1], g1_s.at[di - 1], g1_r.at[di - 1], shifted(di=di))
        for di in range(1, N)
    ]
    for one in g1_copies:
        one.start()
    rs_second(CLOSING[:2])
    lax.fori_loop(0, 3, give_query, 0)
    rs_fill(CLOSING[2:])
    for one in g1_copies:
        one.wait_recv()
    partial = dglb[i].astype(F32)
    for n in range(3):
        partial = partial + g1r[n].astype(F32)
    g2s[0] = partial.astype(BF)
    g2_copies = [
        remote(g2s.at[0], g2r.at[dz - 1], g2_s.at[dz - 1], g2_r.at[dz - 1], shifted(dz=dz)) for dz in range(1, N)
    ]
    for one in g2_copies:
        one.start()
    rs_first(CLOSING[2:])
    lax.fori_loop(3, 4, late, 0)
    lax.fori_loop(3, 4, give_query, 0)
    for one in g2_copies:
        one.wait_recv()
    for n in range(3):
        partial = partial + g2r[n].astype(F32)
    g2s[1] = partial.astype(BF)
    g3r[i] = g2s[1]
    g3_copies = [
        remote(g2s.at[1], g3r.at[i], g3_s.at[di - 1], g3_r.at[di - 1], shifted(di=di)) for di in range(1, N)
    ]
    for one in g3_copies:
        one.start()
    rs_second(CLOSING[2:])
    for one in g3_copies:
        one.wait_recv()
    for shard in range(N):
        remote(dhb.at[0, shard], hrn.at[shard], dn_s.at[shard], dn_r.at[shard], shifted(di=1)).wait_recv()
        remote(dhb.at[1, shard], hrp.at[shard], dp_s.at[shard], dp_r.at[shard], shifted(di=1)).wait_recv()

    out_copies, home = [], []
    for dy in CLOSING:
        shard = lax.rem(y + dy, N)
        rs_copies[1, dy].wait_recv()
        rs_copies[3, dy].wait_recv()

        def close(b, carry, shard=shard, dy=dy):
            block_id = ((z * N + shard) * N + i) * 2 + b
            extra = named(z * 8 + shard * 2 + b)
            for side in range(2):
                total = acc[shard, 2 + b, side] * (SCALE if side == 0 else 1.0) + extra[side]
                total = total + hrn[shard, b, side].astype(F32) + hrp[shard, b, side].astype(F32)
                for n in range(2):
                    total = total + rsr[n, dy, b, side].astype(F32)
                for g in range(2):
                    hit = (jnp.zeros((BLOCK, HDIM), I32) + glob_ref[g]) == block_id
                    total = total + jnp.where(hit, g3r[2 * g + side].astype(F32), 0.0)
                outb[shard, b, side] = total.astype(BF)
            return carry

        lax.fori_loop(0, 2, close, 0)
        for dh in range(2):
            b = lax.rem(h + dh, 2)
            if (dy, dh) == (0, 0):
                home.append(pltpu.make_async_copy(outb.at[shard, b], dkv.at[h * N + y], loc.at[10]))
                home[-1].start()
            else:
                n = YH.index((dy, dh))
                out_copies.append(
                    remote(
                        outb.at[shard, b], dkv.at[h * N + y], out_s.at[n], out_r.at[n], shifted(dy=dy, dh=dh)
                    )
                )
                out_copies[-1].start()
    for one in out_copies + home + [dq_home]:
        one.wait()
    for k in range(1, N):
        dq_copy(k).wait()
    for one in list(kv_copies.values()) + list(q_copies.values()) + it_copies + st_copies:
        one.wait_send()
    for one in list(ag_copies.values()) + list(rs_copies.values()):
        one.wait_send()
    for one in hn_copies + hp_copies + gl_copies + g1_copies + g2_copies + g3_copies:
        one.wait_send()
    for shard in range(N):
        remote(dhb.at[0, shard], hrn.at[shard], dn_s.at[shard], dn_r.at[shard], shifted(di=1)).wait_send()
        remote(dhb.at[1, shard], hrp.at[shard], dp_s.at[shard], dp_r.at[shard], shifted(di=1)).wait_send()


def hand_over(dq, dkv, dq_out, dk_out, dv_out, wide, tall, sems_in, sems_out):
    come = [pltpu.make_async_copy(dq.at[pl.ds(64 * n, 64)], wide.at[n], sems_in.at[n]) for n in range(4)]
    leave = [pltpu.make_async_copy(wide.at[n], dq_out.at[pl.ds(64 * n, 64)], sems_out.at[n]) for n in range(4)]
    whole_in = pltpu.make_async_copy(dkv, tall, sems_in.at[4])
    for one in come:
        one.start()
    whole_in.start()
    for first, then in zip(come, leave):
        first.wait()
        then.start()
    whole_in.wait()
    for n in range(8):
        for side, ref in enumerate((dk_out, dv_out)):
            leave.append(
                pltpu.make_async_copy(
                    tall.at[n, side], ref.at[:, n * HDIM : (n + 1) * HDIM], sems_out.at[4 + 2 * n + side]
                )
            )
            leave[-1].start()
    for one in leave:
        one.wait()


HBM = pl.BlockSpec(memory_space=pltpu.HBM)
SMEM = pl.BlockSpec(memory_space=pltpu.SMEM)
DMA = pltpu.SemaphoreType.DMA


def on_device(
    queries, key_heads, value_heads, output, output_grad, log_totals, random_blocks, window_width, global_blocks
):
    shape = jax.ShapeDtypeStruct
    tile = (BLOCK, HDIM)
    twice = lambda n: [DMA((n,)), DMA((n,))]
    results = pl.pallas_call(
        fused,
        out_shape=(
            shape((256, 2048), BF),
            shape((8, 2) + tile, BF),
        ),
        in_specs=[SMEM, SMEM, SMEM] + [HBM] * 6,
        out_specs=(HBM, HBM),
        scratch_shapes=[
            pltpu.VMEM((2, 256, 2048), BF),
            pltpu.VMEM((16, 256), F32),
            pltpu.VMEM((N, 8, 256), F32),
            pltpu.VMEM((8, 2) + tile, BF),
            pltpu.VMEM((8, 128), I32),
            pltpu.VMEM((N, 8, 128), I32),
            pltpu.SMEM((N, 8, 128), I32),
            pltpu.VMEM((N, 8, 256), F32),
            pltpu.VMEM((N, 256, 512), BF),
            pltpu.VMEM((N, 256, 512), BF),
            pltpu.VMEM((32, 2) + tile, BF),
            pltpu.VMEM((2, N, 2, 2) + tile, BF),
            pltpu.VMEM((2, 2) + tile, BF),
            pltpu.VMEM((N, 2, 2) + tile, BF),
            pltpu.VMEM((8, HDIM, 512), F32),
            pltpu.VMEM((N, 6, 2) + tile, F32),
            pltpu.VMEM((2, N, 2, 2) + tile, BF),
            pltpu.VMEM((N, 2, 2) + tile, BF),
            pltpu.VMEM((N, 2, 2) + tile, BF),
            pltpu.VMEM((N, 7, 2) + tile, BF),
            pltpu.VMEM((3, N, 2, 2) + tile, BF),
            pltpu.VMEM((N, 2, 2) + tile, BF),
            pltpu.VMEM((2, N, 2, 2) + tile, BF),
            pltpu.VMEM((2, 2) + tile, F32),
            pltpu.VMEM((4,) + tile, BF),
            pltpu.VMEM((3,) + tile, BF),
            pltpu.VMEM((2,) + tile, BF),
            pltpu.VMEM((3,) + tile, BF),
            pltpu.VMEM((4,) + tile, BF),
            pltpu.VMEM((N, 256, 512), BF),
            pltpu.VMEM((N, 2, 2) + tile, BF),
            DMA((12,)),
            DMA((16,)),
        ]
        + twice(7) + twice(6) + twice(3) + twice(3) + twice(12) + twice(4) + twice(4) + twice(3)
        + twice(4) + twice(4) + twice(12) + twice(3) + twice(3) + twice(3) + twice(3) + twice(7),
        compiler_params=pltpu.CompilerParams(
            collective_id=0, has_side_effects=True, vmem_limit_bytes=60 * 2**20
        ),
        name="fused",
    )(
        global_blocks, random_blocks, window_width, queries, key_heads, value_heads, output, output_grad, log_totals
    )
    return pl.pallas_call(
        hand_over,
        out_shape=(shape((256, 2048), BF), shape((BLOCK, 1024), BF), shape((BLOCK, 1024), BF)),
        in_specs=[HBM] * 2,
        out_specs=(HBM, HBM, HBM),
        scratch_shapes=[
            pltpu.VMEM((4, 64, 2048), BF),
            pltpu.VMEM((8, 2) + tile, BF),
            DMA((5,)),
            DMA((20,)),
        ],
        compiler_params=pltpu.CompilerParams(vmem_limit_bytes=60 * 2**20),
        name="hand_over",
    )(*results)


def solution(mesh):
    placed = (
        P(("outer", "inner"), "head"),
        P(("outer", "inner", "head"), None),
        P(("outer", "inner", "head"), None),
        P(("outer", "inner"), "head"),
        P(("outer", "inner"), "head"),
        P("head", ("outer", "inner")),
        P(("outer", "inner"), None),
        P(("outer", "inner")),
        P(),
    )
    return jax.shard_map(
        on_device,
        mesh=mesh,
        in_specs=placed,
        out_specs=(
            P(("outer", "inner"), "head"),
            P(("outer", "inner", "head"), None),
            P(("outer", "inner", "head"), None),
        ),
        check_vma=False,
    )
```

```python
import math

import jax
import jax.numpy as jnp
from jax import lax
from jax.experimental import pallas as pl
from jax.experimental.pallas import tpu as pltpu
from jax.sharding import PartitionSpec as P

MESH = pl.DeviceIdType.MESH
HDIM = 128
BLOCK = 128
N = 4
SCALE = HDIM ** (-0.5)
LOG2E = math.log2(math.e)
ORDER = (0, 1, 3, 2)
UPWARD = (0, 3)
WINDOW_GROUPS = ((0, 1), (2, 3), (4,))
RANDOM_GROUPS = ((0, 1), (2,))
CLOSING = (2, 1, 3, 0)
BACKUP = (2, 3)
YH = [(dy, dh) for dy in range(4) for dh in range(2) if (dy, dh) != (0, 0)]
BF = jnp.bfloat16
F32 = jnp.float32
I32 = jnp.int32
NT = (((1,), (1,)), ((), ()))
TN = (((0,), (0,)), ((), ()))


def place():
    outer = lax.axis_index("outer")
    return outer // N, lax.rem(outer, N), lax.axis_index("inner"), lax.axis_index("head")


def device(z, y, i, h):
    return (z * N + y, i, h)


def shifted(dz=0, dy=0, di=0, dh=0):
    z, y, i, h = place()
    return device(lax.rem(z + dz, N), lax.rem(y + dy, N), lax.rem(i + di, N), lax.rem(h + dh, 2))


def following(shard):
    z, y, i, h = place()
    wrap = (i == N - 1).astype(I32)
    spot = lax.rem(shard + wrap, N)
    cross = wrap * jnp.where(shard == N - 1, 1, 0)
    return device(lax.rem(z + cross, N), y, lax.rem(i + 1, N), h), spot


def preceding(shard):
    z, y, i, h = place()
    wrap = (i == 0).astype(I32)
    spot = lax.rem(shard - wrap + N, N)
    cross = wrap * jnp.where(shard == 0, 1, 0)
    return device(lax.rem(z - cross + N, N), y, lax.rem(i + N - 1, N), h), spot


def greet():
    barrier = pltpu.get_barrier_semaphore()
    found = [shifted(dy=dy, dh=dh) for dy, dh in YH]
    found += [shifted(dz=dz) for dz in range(1, N)]
    found += [shifted(di=di) for di in range(1, N)]
    found += [following(N - 1)[0], preceding(0)[0]]
    for one in found:
        pl.semaphore_signal(barrier, inc=1, device_id=one, device_id_type=MESH)
    return barrier, len(found)


def remote(src, dst, send, recv, to):
    return pltpu.make_async_remote_copy(
        src_ref=src, dst_ref=dst, send_sem=send, recv_sem=recv, device_id=to, device_id_type=MESH
    )


def columns(index, width):
    return pl.ds(pl.multiple_of(index * width, width), width)


def offset_of(k):
    if isinstance(k, int):
        return (0, 1, 3, 2)[k]
    return k + (k == 2).astype(I32) - (k == 3).astype(I32)


def block_slot(block):
    shard = block // 2
    return (shard // (N * N)) * 8 + lax.rem(shard // N, N) * 2 + lax.rem(block, 2)


def fused(
    glob_ref, rand_ref, width_ref, q_ref, k_ref, v_ref, o_ref, g_ref, lse_ref,
    dq, dkv,
    og, lseb, sbuf, kvh, intb, intr, ints, stats, qb, gb, kvu, hal, gsend, grecv,
    dqt, dsb, acc, dhb, hrn, hrp, ent, rsb, rst, rsr, gacc, dglb, g1r, g2s, g2r, g3r, dqb, outb,
    loc, kvl, kv_s, kv_r, q_s, q_r, st_s, st_r, it_s, it_r, ag_s, ag_r, hn_s, hn_r, hp_s, hp_r, gl_s, gl_r,
    dn_s, dn_r, dp_s, dp_r, rs_s, rs_r, g1_s, g1_r, g2_s, g2_r, g3_s, g3_r, dq_s, dq_r, out_s, out_r,
):
    z, y, i, h = place()
    own_slot = z * 8 + y * 2 + h
    own_col = columns(h * N + y, HDIM)
    loads = [
        pltpu.make_async_copy(o_ref, og.at[0], loc.at[0]),
        pltpu.make_async_copy(g_ref, og.at[1], loc.at[1]),
        pltpu.make_async_copy(lse_ref, lseb, loc.at[2]),
    ]
    keep = [
        pltpu.make_async_copy(k_ref.at[:, own_col], kvu.at[own_slot, 0], loc.at[3]),
        pltpu.make_async_copy(v_ref.at[:, own_col], kvu.at[own_slot, 1], loc.at[4]),
    ]
    stay = [
        pltpu.make_async_copy(q_ref.at[:, columns(y, 512)], qb.at[y], loc.at[5]),
        pltpu.make_async_copy(g_ref.at[:, columns(y, 512)], gb.at[y], loc.at[6]),
    ]
    staged = []
    for n in range(8):
        for side, ref in enumerate((k_ref, v_ref)):
            staged.append(
                pltpu.make_async_copy(ref.at[:, n * HDIM : (n + 1) * HDIM], kvh.at[n, side], kvl.at[2 * n + side])
            )
    for one in staged + keep + loads + stay:
        one.start()
    lane = lax.broadcasted_iota(I32, (8, 128), 1)
    sub = lax.broadcasted_iota(I32, (8, 128), 0)
    row = jnp.zeros((8, 128), I32)
    for b in range(2):
        for r in range(3):
            slot = block_slot(rand_ref[b, r])
            row = jnp.where((lane == b * 3 + r) & (sub == 0), slot, row)
            row = jnp.where((lane == slot) & (sub == 1), b * 3 + r + 1, row)
        row = jnp.where((lane == 6 + b) & (sub == 0), width_ref[b], row)
    intb[...] = row
    barrier, arrivals = greet()
    pl.semaphore_wait(barrier, arrivals)

    it_copies = [
        remote(intb, intr.at[y], it_s.at[dy - 1], it_r.at[dy - 1], shifted(dy=dy)) for dy in range(1, N)
    ]
    kv_copies = {}
    for one in staged:
        one.wait()
    for dy, dh in sorted(YH, key=lambda s: ((0, 1, 3, 2)[s[0]], s[1])):
        n = YH.index((dy, dh))
        to = shifted(dy=dy, dh=dh)
        part = lax.rem(h + dh, 2) * N + lax.rem(y + dy, N)
        kv_copies[dy, dh] = remote(kvh.at[part], kvu.at[own_slot], kv_s.at[n], kv_r.at[n], to)
        kv_copies[dy, dh].start()
    for one in it_copies:
        one.start()
    intr[y] = row
    for one in loads:
        one.wait()
    picker = (
        lax.broadcasted_iota(I32, (8, 512), 1) // HDIM == lax.broadcasted_iota(I32, (8, 512), 0) - 4
    ).astype(BF)
    for c in range(N):
        prod = og[0, :, c * 512 : (c + 1) * 512].astype(F32) * og[1, :, c * 512 : (c + 1) * 512].astype(F32)
        high = prod.astype(BF)
        low = (prod - high.astype(F32)).astype(BF)
        delta = lax.dot_general(picker, high, NT, preferred_element_type=F32)
        delta = delta + lax.dot_general(picker, low, NT, preferred_element_type=F32)
        sbuf[c] = jnp.concatenate([lseb[4 * c : 4 * c + 4, :] * LOG2E, delta[4:8]], axis=0)
    st_copies = [
        remote(sbuf.at[lax.rem(y + dy, N)], stats.at[y], st_s.at[dy - 1], st_r.at[dy - 1], shifted(dy=dy))
        for dy in range(1, N)
    ]
    for one in st_copies:
        one.start()
    own_stats = pltpu.make_async_copy(sbuf.at[y], stats.at[y], loc.at[7])
    own_stats.start()
    q_copies = {}

    def ask(dy):
        c = lax.rem(y + dy, N)
        for side, (ref, dst) in enumerate(((q_ref, qb), (g_ref, gb))):
            n = 2 * (dy - 1) + side
            q_copies[dy, side] = remote(
                ref.at[:, columns(c, 512)], dst.at[y], q_s.at[n], q_r.at[n], shifted(dy=dy)
            )
            q_copies[dy, side].start()

    ask(1)
    for one in keep:
        one.wait()

    ag_copies, hn_copies, hp_copies = {}, [], []

    def spread(dy):
        shard = lax.rem(y - dy + N, N)
        for dh in range(2):
            if (dy, dh) != (0, 0):
                kv_copies[dy, dh].wait_recv()
        here = pl.ds(pl.multiple_of(z * 8 + shard * 2, 2), 2)
        for dz in (1, 3):
            n = dy * 3 + dz - 1
            ag_copies[dy, dz] = remote(kvu.at[here], kvu.at[here], ag_s.at[n], ag_r.at[n], shifted(dz=dz))
            ag_copies[dy, dz].start()
        to, spot = following(shard)
        hn_copies.append(remote(kvu.at[here], hal.at[0, spot], hn_s.at[dy], hn_r.at[spot], to))
        hn_copies[-1].start()
        to, spot = preceding(shard)
        hp_copies.append(remote(kvu.at[here], hal.at[1, spot], hp_s.at[dy], hp_r.at[spot], to))
        hp_copies[-1].start()

    def pass_on(dy):
        step = 1 if dy in UPWARD else 3
        ag_copies[dy, step].wait_recv()
        shard = lax.rem(y - dy + N, N)
        here = pl.ds(pl.multiple_of(lax.rem(z - step + N, N) * 8 + shard * 2, 2), 2)
        n = dy * 3 + 1
        ag_copies[dy, 2] = remote(kvu.at[here], kvu.at[here], ag_s.at[n], ag_r.at[n], shifted(dz=step))
        ag_copies[dy, 2].start()

    spread(0)
    ask(3)
    spread(1)
    pass_on(0)
    spread(3)
    pass_on(1)
    spread(2)
    for one in it_copies + st_copies:
        one.wait_recv()
    own_stats.wait()
    to_scalar = pltpu.make_async_copy(intr, ints, loc.at[8])
    to_scalar.start()
    to_scalar.wait()
    for shard in range(N):
        ent[shard, 0] = jnp.zeros((2, BLOCK, HDIM), BF)
    for g in range(2):
        for side in range(2):
            gacc[g, side] = jnp.zeros((BLOCK, HDIM), F32)

    def load_block(shard, b):
        rows = slice(b * BLOCK, (b + 1) * BLOCK)
        query = jnp.concatenate([qb[shard, rows, j * HDIM : (j + 1) * HDIM] for j in range(4)], axis=0)
        grad = jnp.concatenate([gb[shard, rows, j * HDIM : (j + 1) * HDIM] for j in range(4)], axis=0)
        tile = stats[shard, :, rows]
        lse = jnp.concatenate([tile[j : j + 1] for j in range(4)], axis=1)
        delta = jnp.concatenate([tile[4 + j : 5 + j] for j in range(4)], axis=1)
        return query, grad, lse, delta

    def attend(pairs, lses, query, grad, delta, held=None):
        count = len(pairs)
        keys = jnp.concatenate([k for k, _ in pairs], axis=0)
        values = jnp.concatenate([v for _, v in pairs], axis=0)
        scores = lax.dot_general(keys, query, NT, preferred_element_type=F32) * (SCALE * LOG2E)
        scores = jnp.concatenate([scores[k * BLOCK : (k + 1) * BLOCK] - lses[k] for k in range(count)], axis=0)
        probs = jnp.exp2(scores)
        prob_grad = lax.dot_general(values, grad, NT, preferred_element_type=F32)
        score_grad = (probs * (prob_grad - delta)).astype(BF)
        value_entry = jnp.dot(probs.astype(BF), grad, preferred_element_type=F32)
        key_entry = jnp.dot(score_grad, query, preferred_element_type=F32)
        if held is None:
            turned = lax.dot_general(keys, score_grad, TN, preferred_element_type=F32)
        else:
            block, start = held
            dsb[block, start : start + count * BLOCK] = score_grad
            turned = None
        cut = [slice(k * BLOCK, (k + 1) * BLOCK) for k in range(count)]
        return [key_entry[c] for c in cut], [value_entry[c] for c in cut], turned

    def window(k, add):
        shard = lax.rem(y - offset_of(k) + N, N)
        remote(hal.at[0, shard], hal.at[0, shard], hn_s.at[shard], hn_r.at[shard], shifted(di=1)).wait_recv()
        remote(hal.at[1, shard], hal.at[1, shard], hp_s.at[shard], hp_r.at[shard], shifted(di=1)).wait_recv()
        for b in range(2):
            query, grad, lse, delta = load_block(shard, b)
            width = ints[shard, 0, 6 + b]
            block_id = ((z * N + shard) * N + i) * 2 + b
            total = None
            for group in WINDOW_GROUPS:
                pairs, lses = [], []
                for e in group:
                    at = b + e - 2
                    if at < 0:
                        pairs.append((hal[0, shard, at + 2, 0], hal[0, shard, at + 2, 1]))
                    elif at >= 2:
                        pairs.append((hal[1, shard, at - 2, 0], hal[1, shard, at - 2, 1]))
                    else:
                        slot = z * 8 + shard * 2 + at
                        pairs.append((kvu[slot, 0], kvu[slot, 1]))
                    target = block_id + e - 2
                    ok = (abs(e - 2) <= width) & (target >= 0) & (target < 128)
                    lses.append(lse + jnp.where(ok, 0.0, 1e6).astype(F32))
                dks, dvs, turned = attend(pairs, lses, query, grad, delta)
                total = turned if total is None else total + turned
                for e, dk_e, dv_e in zip(group, dks, dvs):
                    at = b + e
                    if b == 0 or at == 5:
                        acc[shard, at, 0] = dk_e
                        acc[shard, at, 1] = dv_e
                    else:
                        acc[shard, at, 0] += dk_e
                        acc[shard, at, 1] += dv_e
            if add:
                dqt[2 * k + b] += total
            else:
                dqt[2 * k + b] = total
        for n, start in enumerate((0, 4)):
            for b in range(2):
                dhb[n, shard, b, 0] = (acc[shard, start + b, 0] * SCALE).astype(BF)
                dhb[n, shard, b, 1] = acc[shard, start + b, 1].astype(BF)
        to, spot = preceding(shard)
        remote(dhb.at[0, shard], hrn.at[spot], dn_s.at[shard], dn_r.at[spot], to).start()
        to, spot = following(shard)
        remote(dhb.at[1, shard], hrp.at[spot], dp_s.at[shard], dp_r.at[spot], to).start()

    def wait_queries(k):
        dy = offset_of(k)
        for side, (ref, dst) in enumerate(((q_ref, qb), (g_ref, gb))):
            n = 2 * (dy - 1) + side
            remote(
                ref.at[:, columns(y, 512)], dst.at[y], q_s.at[n], q_r.at[n], shifted(dy=1)
            ).wait_recv()

    for one in stay:
        one.wait()
    def early(k, carry):
        @pl.when(k > 0)
        def _():
            wait_queries(k)

        window(k, False)
        return carry

    lax.fori_loop(0, 1, early, 0)
    ask(2)
    pass_on(3)
    pass_on(2)
    lax.fori_loop(1, 3, early, 0)

    for dy in range(N):
        for dz in range(1, N):
            if dz == 2 or dz == (3 if dy in UPWARD else 1):
                ag_copies[dy, dz].wait_recv()
    for g in range(2):
        gsend[g] = kvu[block_slot(glob_ref[g])]
    gl_copies = [
        remote(gsend, grecv.at[di], gl_s.at[di - 1], gl_r.at[di - 1], shifted(di=di)) for di in range(1, N)
    ]
    for one in gl_copies:
        one.start()
    grecv[0] = gsend[...]

    def random(k, carry):
        @pl.when(k == 3)
        def _():
            wait_queries(k)

        shard = lax.rem(y - offset_of(k) + N, N)
        for b in range(2):
            query, grad, lse, delta = load_block(shard, b)
            for group in RANDOM_GROUPS:
                slots = [ints[shard, 0, b * 3 + r] for r in group]
                pairs = [(kvu[s, 0], kvu[s, 1]) for s in slots]
                held = (2 * k + b, (2 + group[0]) * BLOCK)
                dks, dvs, _ = attend(pairs, [lse] * len(group), query, grad, delta, held)
                for r, dk_e, dv_e in zip(group, dks, dvs):
                    ent[shard, 1 + b * 3 + r, 0] = (dk_e * SCALE).astype(BF)
                    ent[shard, 1 + b * 3 + r, 1] = dv_e.astype(BF)
        return carry

    lax.fori_loop(0, N, random, 0)

    def named(slot):
        total = None
        for shard in range(N):
            one = ent[shard, ints[shard, 1, slot]].astype(F32)
            total = one if total is None else total + one
        return total

    rs_copies = {}

    def fill(dz, dy):
        shard = lax.rem(y + dy, N)
        to = lax.rem(z + dz, N)

        def put(b, carry):
            rsb[dz - 1, dy, b] = named(to * 8 + shard * 2 + b).astype(BF)
            return carry

        lax.fori_loop(0, 2, put, 0)

    def rs_send(dz, dy, dst, to):
        n = dy * 3 + dz - 1
        rs_copies[dz, dy] = remote(rsb.at[dz - 1, dy], dst, rs_s.at[n], rs_r.at[n], to)
        rs_copies[dz, dy].start()

    def rs_fill(dys):
        for dy in dys:
            fill(2, dy)
        for dy in dys:
            fill(3 if dy in BACKUP else 1, dy)
        for dy in dys:
            fill(1 if dy in BACKUP else 3, dy)

    def rs_first(dys):
        for dy in dys:
            rs_send(2, dy, rst.at[dy], shifted(dz=1 if dy in BACKUP else 3))
        for dy in dys:
            dz = 3 if dy in BACKUP else 1
            rs_send(dz, dy, rsr.at[dz // 2, dy], shifted(dz=dz))

    def rs_second(dys):
        for dy in dys:
            dz = 1 if dy in BACKUP else 3
            rs_copies[2, dy].wait_recv()

            def join(b, carry, dz=dz, dy=dy):
                rsb[dz - 1, dy, b] = (rsb[dz - 1, dy, b].astype(F32) + rst[dy, b].astype(F32)).astype(BF)
                return carry

            lax.fori_loop(0, 2, join, 0)
            rs_send(dz, dy, rsr.at[dz // 2, dy], shifted(dz=dz))

    rs_fill(CLOSING[:2])
    rs_first(CLOSING[:2])

    for one in gl_copies:
        one.wait_recv()
    globe = []
    for g in range(2):
        source = lax.rem(i - lax.rem(glob_ref[g] // 2, N) + N, N)
        globe.append(source)

    def dq_copy(k):
        dy = offset_of(k)
        shard = lax.rem(y - dy + N, N)
        return remote(
            dqb.at[shard], dq.at[:, columns(y, 512)], dq_s.at[dy - 1], dq_r.at[dy - 1], device(z, shard, i, h)
        )

    dq_home = pltpu.make_async_copy(dqb.at[y], dq.at[:, columns(y, 512)], loc.at[9])

    def whole(k, carry):
        shard = lax.rem(y - offset_of(k) + N, N)
        for b in range(2):
            query, grad, lse, delta = load_block(shard, b)
            pairs = [(grecv[globe[g], g, 0], grecv[globe[g], g, 1]) for g in range(2)]
            dks, dvs, _ = attend(pairs, [lse] * 2, query, grad, delta, (2 * k + b, 0))
            for g in range(2):
                gacc[g, 0] += dks[g]
                gacc[g, 1] += dvs[g]
        return carry

    def give_query(k, carry):
        shard = lax.rem(y - offset_of(k) + N, N)
        for b in range(2):
            keys = [grecv[globe[g], g, 0] for g in range(2)]
            keys += [kvu[ints[shard, 0, b * 3 + r], 0] for r in range(3)]
            turned = lax.dot_general(
                jnp.concatenate(keys, axis=0), dsb[2 * k + b], TN, preferred_element_type=F32
            )
            done = (jnp.transpose(dqt[2 * k + b] + turned) * SCALE).astype(BF)
            for j in range(4):
                dqb[shard, b * BLOCK : (b + 1) * BLOCK, j * HDIM : (j + 1) * HDIM] = done[
                    j * BLOCK : (j + 1) * BLOCK
                ]

        @pl.when(k == 0)
        def _():
            dq_home.start()

        @pl.when(k > 0)
        def _():
            dq_copy(k).start()

        return carry

    def late(k, carry):
        window(k, False)
        return carry

    lax.fori_loop(0, N, whole, 0)
    for g in range(2):
        dglb[2 * g] = (gacc[g, 0] * SCALE).astype(BF)
        dglb[2 * g + 1] = gacc[g, 1].astype(BF)
    g1_copies = [
        remote(dglb.at[lax.rem(i + di, N)], g1r.at[di - 1], g1_s.at[di - 1], g1_r.at[di - 1], shifted(di=di))
        for di in range(1, N)
    ]
    for one in g1_copies:
        one.start()
    rs_second(CLOSING[:2])
    lax.fori_loop(0, 3, give_query, 0)
    rs_fill(CLOSING[2:])
    for one in g1_copies:
        one.wait_recv()
    partial = dglb[i].astype(F32)
    for n in range(3):
        partial = partial + g1r[n].astype(F32)
    g2s[0] = partial.astype(BF)
    g2_copies = [
        remote(g2s.at[0], g2r.at[dz - 1], g2_s.at[dz - 1], g2_r.at[dz - 1], shifted(dz=dz)) for dz in range(1, N)
    ]
    for one in g2_copies:
        one.start()
    rs_first(CLOSING[2:])
    lax.fori_loop(3, 4, late, 0)
    lax.fori_loop(3, 4, give_query, 0)
    for one in g2_copies:
        one.wait_recv()
    for n in range(3):
        partial = partial + g2r[n].astype(F32)
    g2s[1] = partial.astype(BF)
    g3r[i] = g2s[1]
    g3_copies = [
        remote(g2s.at[1], g3r.at[i], g3_s.at[di - 1], g3_r.at[di - 1], shifted(di=di)) for di in range(1, N)
    ]
    for one in g3_copies:
        one.start()
    rs_second(CLOSING[2:])
    for one in g3_copies:
        one.wait_recv()
    for shard in range(N):
        remote(dhb.at[0, shard], hrn.at[shard], dn_s.at[shard], dn_r.at[shard], shifted(di=1)).wait_recv()
        remote(dhb.at[1, shard], hrp.at[shard], dp_s.at[shard], dp_r.at[shard], shifted(di=1)).wait_recv()

    out_copies, home = [], []
    for dy in CLOSING:
        shard = lax.rem(y + dy, N)
        rs_copies[1, dy].wait_recv()
        rs_copies[3, dy].wait_recv()

        def close(b, carry, shard=shard, dy=dy):
            block_id = ((z * N + shard) * N + i) * 2 + b
            extra = named(z * 8 + shard * 2 + b)
            for side in range(2):
                total = acc[shard, 2 + b, side] * (SCALE if side == 0 else 1.0) + extra[side]
                total = total + hrn[shard, b, side].astype(F32) + hrp[shard, b, side].astype(F32)
                for n in range(2):
                    total = total + rsr[n, dy, b, side].astype(F32)
                for g in range(2):
                    hit = (jnp.zeros((BLOCK, HDIM), I32) + glob_ref[g]) == block_id
                    total = total + jnp.where(hit, g3r[2 * g + side].astype(F32), 0.0)
                outb[shard, b, side] = total.astype(BF)
            return carry

        lax.fori_loop(0, 2, close, 0)
        for dh in range(2):
            b = lax.rem(h + dh, 2)
            if (dy, dh) == (0, 0):
                home.append(pltpu.make_async_copy(outb.at[shard, b], dkv.at[h * N + y], loc.at[10]))
                home[-1].start()
            else:
                n = YH.index((dy, dh))
                out_copies.append(
                    remote(
                        outb.at[shard, b], dkv.at[h * N + y], out_s.at[n], out_r.at[n], shifted(dy=dy, dh=dh)
                    )
                )
                out_copies[-1].start()
    for one in out_copies + home + [dq_home]:
        one.wait()
    for k in range(1, N):
        dq_copy(k).wait()
    for one in list(kv_copies.values()) + list(q_copies.values()) + it_copies + st_copies:
        one.wait_send()
    for one in list(ag_copies.values()) + list(rs_copies.values()):
        one.wait_send()
    for one in hn_copies + hp_copies + gl_copies + g1_copies + g2_copies + g3_copies:
        one.wait_send()
    for shard in range(N):
        remote(dhb.at[0, shard], hrn.at[shard], dn_s.at[shard], dn_r.at[shard], shifted(di=1)).wait_send()
        remote(dhb.at[1, shard], hrp.at[shard], dp_s.at[shard], dp_r.at[shard], shifted(di=1)).wait_send()


def hand_over(dq, dkv, dq_out, dk_out, dv_out, wide, tall, sems_in, sems_out):
    come = [pltpu.make_async_copy(dq.at[pl.ds(64 * n, 64)], wide.at[n], sems_in.at[n]) for n in range(4)]
    leave = [pltpu.make_async_copy(wide.at[n], dq_out.at[pl.ds(64 * n, 64)], sems_out.at[n]) for n in range(4)]
    whole_in = pltpu.make_async_copy(dkv, tall, sems_in.at[4])
    for one in come:
        one.start()
    whole_in.start()
    for first, then in zip(come, leave):
        first.wait()
        then.start()
    whole_in.wait()
    for n in range(8):
        for side, ref in enumerate((dk_out, dv_out)):
            leave.append(
                pltpu.make_async_copy(
                    tall.at[n, side], ref.at[:, n * HDIM : (n + 1) * HDIM], sems_out.at[4 + 2 * n + side]
                )
            )
            leave[-1].start()
    for one in leave:
        one.wait()


HBM = pl.BlockSpec(memory_space=pltpu.HBM)
SMEM = pl.BlockSpec(memory_space=pltpu.SMEM)
DMA = pltpu.SemaphoreType.DMA


def on_device(
    queries, key_heads, value_heads, output, output_grad, log_totals, random_blocks, window_width, global_blocks
):
    shape = jax.ShapeDtypeStruct
    tile = (BLOCK, HDIM)
    twice = lambda n: [DMA((n,)), DMA((n,))]
    results = pl.pallas_call(
        fused,
        out_shape=(
            shape((256, 2048), BF),
            shape((8, 2) + tile, BF),
        ),
        in_specs=[SMEM, SMEM, SMEM] + [HBM] * 6,
        out_specs=(HBM, HBM),
        scratch_shapes=[
            pltpu.VMEM((2, 256, 2048), BF),
            pltpu.VMEM((16, 256), F32),
            pltpu.VMEM((N, 8, 256), F32),
            pltpu.VMEM((8, 2) + tile, BF),
            pltpu.VMEM((8, 128), I32),
            pltpu.VMEM((N, 8, 128), I32),
            pltpu.SMEM((N, 8, 128), I32),
            pltpu.VMEM((N, 8, 256), F32),
            pltpu.VMEM((N, 256, 512), BF),
            pltpu.VMEM((N, 256, 512), BF),
            pltpu.VMEM((32, 2) + tile, BF),
            pltpu.VMEM((2, N, 2, 2) + tile, BF),
            pltpu.VMEM((2, 2) + tile, BF),
            pltpu.VMEM((N, 2, 2) + tile, BF),
            pltpu.VMEM((8, HDIM, 512), F32),
            pltpu.VMEM((8, 5 * BLOCK, 512), BF),
            pltpu.VMEM((N, 6, 2) + tile, F32),
            pltpu.VMEM((2, N, 2, 2) + tile, BF),
            pltpu.VMEM((N, 2, 2) + tile, BF),
            pltpu.VMEM((N, 2, 2) + tile, BF),
            pltpu.VMEM((N, 7, 2) + tile, BF),
            pltpu.VMEM((3, N, 2, 2) + tile, BF),
            pltpu.VMEM((N, 2, 2) + tile, BF),
            pltpu.VMEM((2, N, 2, 2) + tile, BF),
            pltpu.VMEM((2, 2) + tile, F32),
            pltpu.VMEM((4,) + tile, BF),
            pltpu.VMEM((3,) + tile, BF),
            pltpu.VMEM((2,) + tile, BF),
            pltpu.VMEM((3,) + tile, BF),
            pltpu.VMEM((4,) + tile, BF),
            pltpu.VMEM((N, 256, 512), BF),
            pltpu.VMEM((N, 2, 2) + tile, BF),
            DMA((12,)),
            DMA((16,)),
        ]
        + twice(7) + twice(6) + twice(3) + twice(3) + twice(12) + twice(4) + twice(4) + twice(3)
        + twice(4) + twice(4) + twice(12) + twice(3) + twice(3) + twice(3) + twice(3) + twice(7),
        compiler_params=pltpu.CompilerParams(
            collective_id=0, has_side_effects=True, vmem_limit_bytes=60 * 2**20
        ),
        name="fused",
    )(
        global_blocks, random_blocks, window_width, queries, key_heads, value_heads, output, output_grad, log_totals
    )
    return pl.pallas_call(
        hand_over,
        out_shape=(shape((256, 2048), BF), shape((BLOCK, 1024), BF), shape((BLOCK, 1024), BF)),
        in_specs=[HBM] * 2,
        out_specs=(HBM, HBM, HBM),
        scratch_shapes=[
            pltpu.VMEM((4, 64, 2048), BF),
            pltpu.VMEM((8, 2) + tile, BF),
            DMA((5,)),
            DMA((20,)),
        ],
        compiler_params=pltpu.CompilerParams(vmem_limit_bytes=60 * 2**20),
        name="hand_over",
    )(*results)


def solution(mesh):
    placed = (
        P(("outer", "inner"), "head"),
        P(("outer", "inner", "head"), None),
        P(("outer", "inner", "head"), None),
        P(("outer", "inner"), "head"),
        P(("outer", "inner"), "head"),
        P("head", ("outer", "inner")),
        P(("outer", "inner"), None),
        P(("outer", "inner")),
        P(),
    )
    return jax.shard_map(
        on_device,
        mesh=mesh,
        in_specs=placed,
        out_specs=(
            P(("outer", "inner"), "head"),
            P(("outer", "inner", "head"), None),
            P(("outer", "inner", "head"), None),
        ),
        check_vma=False,
    )
```

```python
import math

import jax
import jax.numpy as jnp
from jax import lax
from jax.experimental import pallas as pl
from jax.experimental.pallas import tpu as pltpu
from jax.sharding import PartitionSpec as P

MESH = pl.DeviceIdType.MESH
HDIM = 128
BLOCK = 128
N = 4
SCALE = HDIM ** (-0.5)
LOG2E = math.log2(math.e)
ORDER = (0, 1, 3, 2)
UPWARD = (0, 3)
WINDOW_GROUPS = ((0, 1), (2, 3), (4,))
RANDOM_GROUPS = ((0, 1), (2,))
CLOSING = (2, 1, 3, 0)
YH = [(dy, dh) for dy in range(4) for dh in range(2) if (dy, dh) != (0, 0)]
BF = jnp.bfloat16
F32 = jnp.float32
I32 = jnp.int32
NT = (((1,), (1,)), ((), ()))
TN = (((0,), (0,)), ((), ()))


def place():
    outer = lax.axis_index("outer")
    return outer // N, lax.rem(outer, N), lax.axis_index("inner"), lax.axis_index("head")


def device(z, y, i, h):
    return (z * N + y, i, h)


def shifted(dz=0, dy=0, di=0, dh=0):
    z, y, i, h = place()
    return device(lax.rem(z + dz, N), lax.rem(y + dy, N), lax.rem(i + di, N), lax.rem(h + dh, 2))


def following(shard):
    z, y, i, h = place()
    wrap = (i == N - 1).astype(I32)
    spot = lax.rem(shard + wrap, N)
    cross = wrap * jnp.where(shard == N - 1, 1, 0)
    return device(lax.rem(z + cross, N), y, lax.rem(i + 1, N), h), spot


def preceding(shard):
    z, y, i, h = place()
    wrap = (i == 0).astype(I32)
    spot = lax.rem(shard - wrap + N, N)
    cross = wrap * jnp.where(shard == 0, 1, 0)
    return device(lax.rem(z - cross + N, N), y, lax.rem(i + N - 1, N), h), spot


def greet():
    barrier = pltpu.get_barrier_semaphore()
    found = [shifted(dy=dy, dh=dh) for dy, dh in YH]
    found += [shifted(dz=dz) for dz in range(1, N)]
    found += [shifted(di=di) for di in range(1, N)]
    found += [following(N - 1)[0], preceding(0)[0]]
    for one in found:
        pl.semaphore_signal(barrier, inc=1, device_id=one, device_id_type=MESH)
    return barrier, len(found)


def remote(src, dst, send, recv, to):
    return pltpu.make_async_remote_copy(
        src_ref=src, dst_ref=dst, send_sem=send, recv_sem=recv, device_id=to, device_id_type=MESH
    )


def columns(index, width):
    return pl.ds(pl.multiple_of(index * width, width), width)


def offset_of(k):
    if isinstance(k, int):
        return (0, 1, 3, 2)[k]
    return k + (k == 2).astype(I32) - (k == 3).astype(I32)


def block_slot(block):
    shard = block // 2
    return (shard // (N * N)) * 8 + lax.rem(shard // N, N) * 2 + lax.rem(block, 2)


def fused(
    glob_ref, rand_ref, width_ref, q_ref, k_ref, v_ref, o_ref, g_ref, lse_ref,
    dq, dkv,
    og, lseb, sbuf, kvh, intb, intr, ints, stats, qb, gb, kvu, hal, gsend, grecv,
    dqt, acc, dhb, hrn, hrp, ent, rsb, rsr, gacc, dglb, g1r, g2s, g2r, g3r, dqb, outb,
    loc, kvl, kv_s, kv_r, q_s, q_r, st_s, st_r, it_s, it_r, ag_s, ag_r, hn_s, hn_r, hp_s, hp_r, gl_s, gl_r,
    dn_s, dn_r, dp_s, dp_r, rs_s, rs_r, g1_s, g1_r, g2_s, g2_r, g3_s, g3_r, dq_s, dq_r, out_s, out_r,
):
    z, y, i, h = place()
    own_slot = z * 8 + y * 2 + h
    own_col = columns(h * N + y, HDIM)
    loads = [
        pltpu.make_async_copy(o_ref, og.at[0], loc.at[0]),
        pltpu.make_async_copy(g_ref, og.at[1], loc.at[1]),
        pltpu.make_async_copy(lse_ref, lseb, loc.at[2]),
    ]
    keep = [
        pltpu.make_async_copy(k_ref.at[:, own_col], kvu.at[own_slot, 0], loc.at[3]),
        pltpu.make_async_copy(v_ref.at[:, own_col], kvu.at[own_slot, 1], loc.at[4]),
    ]
    stay = [
        pltpu.make_async_copy(q_ref.at[:, columns(y, 512)], qb.at[y], loc.at[5]),
        pltpu.make_async_copy(g_ref.at[:, columns(y, 512)], gb.at[y], loc.at[6]),
    ]
    staged = []
    for n in range(8):
        for side, ref in enumerate((k_ref, v_ref)):
            staged.append(
                pltpu.make_async_copy(ref.at[:, n * HDIM : (n + 1) * HDIM], kvh.at[n, side], kvl.at[2 * n + side])
            )
    for one in staged + keep + loads + stay:
        one.start()
    lane = lax.broadcasted_iota(I32, (8, 128), 1)
    sub = lax.broadcasted_iota(I32, (8, 128), 0)
    row = jnp.zeros((8, 128), I32)
    for b in range(2):
        for r in range(3):
            slot = block_slot(rand_ref[b, r])
            row = jnp.where((lane == b * 3 + r) & (sub == 0), slot, row)
            row = jnp.where((lane == slot) & (sub == 1), b * 3 + r + 1, row)
        row = jnp.where((lane == 6 + b) & (sub == 0), width_ref[b], row)
    intb[...] = row
    barrier, arrivals = greet()
    pl.semaphore_wait(barrier, arrivals)

    it_copies = [
        remote(intb, intr.at[y], it_s.at[dy - 1], it_r.at[dy - 1], shifted(dy=dy)) for dy in range(1, N)
    ]
    kv_copies = {}
    for one in staged:
        one.wait()
    for dy, dh in sorted(YH, key=lambda s: ((0, 1, 3, 2)[s[0]], s[1])):
        n = YH.index((dy, dh))
        to = shifted(dy=dy, dh=dh)
        part = lax.rem(h + dh, 2) * N + lax.rem(y + dy, N)
        kv_copies[dy, dh] = remote(kvh.at[part], kvu.at[own_slot], kv_s.at[n], kv_r.at[n], to)
        kv_copies[dy, dh].start()
    for one in it_copies:
        one.start()
    intr[y] = row
    for one in loads:
        one.wait()
    picker = (
        lax.broadcasted_iota(I32, (8, 512), 1) // HDIM == lax.broadcasted_iota(I32, (8, 512), 0) - 4
    ).astype(BF)
    for c in range(N):
        prod = og[0, :, c * 512 : (c + 1) * 512].astype(F32) * og[1, :, c * 512 : (c + 1) * 512].astype(F32)
        high = prod.astype(BF)
        low = (prod - high.astype(F32)).astype(BF)
        delta = lax.dot_general(picker, high, NT, preferred_element_type=F32)
        delta = delta + lax.dot_general(picker, low, NT, preferred_element_type=F32)
        sbuf[c] = jnp.concatenate([lseb[4 * c : 4 * c + 4, :] * LOG2E, delta[4:8]], axis=0)
    st_copies = [
        remote(sbuf.at[lax.rem(y + dy, N)], stats.at[y], st_s.at[dy - 1], st_r.at[dy - 1], shifted(dy=dy))
        for dy in range(1, N)
    ]
    for one in st_copies:
        one.start()
    own_stats = pltpu.make_async_copy(sbuf.at[y], stats.at[y], loc.at[7])
    own_stats.start()
    q_copies = {}

    def ask(dy):
        c = lax.rem(y + dy, N)
        for side, (ref, dst) in enumerate(((q_ref, qb), (g_ref, gb))):
            n = 2 * (dy - 1) + side
            q_copies[dy, side] = remote(
                ref.at[:, columns(c, 512)], dst.at[y], q_s.at[n], q_r.at[n], shifted(dy=dy)
            )
            q_copies[dy, side].start()

    ask(1)
    for one in keep:
        one.wait()

    ag_copies, hn_copies, hp_copies = {}, [], []

    def spread(dy):
        shard = lax.rem(y - dy + N, N)
        for dh in range(2):
            if (dy, dh) != (0, 0):
                kv_copies[dy, dh].wait_recv()
        here = pl.ds(pl.multiple_of(z * 8 + shard * 2, 2), 2)
        for dz in (1, 3):
            n = dy * 3 + dz - 1
            ag_copies[dy, dz] = remote(kvu.at[here], kvu.at[here], ag_s.at[n], ag_r.at[n], shifted(dz=dz))
            ag_copies[dy, dz].start()
        to, spot = following(shard)
        hn_copies.append(remote(kvu.at[here], hal.at[0, spot], hn_s.at[dy], hn_r.at[spot], to))
        hn_copies[-1].start()
        to, spot = preceding(shard)
        hp_copies.append(remote(kvu.at[here], hal.at[1, spot], hp_s.at[dy], hp_r.at[spot], to))
        hp_copies[-1].start()

    def pass_on(dy):
        step = 1 if dy in UPWARD else 3
        ag_copies[dy, step].wait_recv()
        shard = lax.rem(y - dy + N, N)
        here = pl.ds(pl.multiple_of(lax.rem(z - step + N, N) * 8 + shard * 2, 2), 2)
        n = dy * 3 + 1
        ag_copies[dy, 2] = remote(kvu.at[here], kvu.at[here], ag_s.at[n], ag_r.at[n], shifted(dz=step))
        ag_copies[dy, 2].start()

    spread(0)
    ask(3)
    spread(1)
    pass_on(0)
    spread(3)
    pass_on(1)
    spread(2)
    for one in it_copies + st_copies:
        one.wait_recv()
    own_stats.wait()
    to_scalar = pltpu.make_async_copy(intr, ints, loc.at[8])
    to_scalar.start()
    to_scalar.wait()
    for shard in range(N):
        ent[shard, 0] = jnp.zeros((2, BLOCK, HDIM), BF)
    for b in range(2):
        dqt[6 + b] = jnp.zeros((HDIM, 512), F32)
    for g in range(2):
        for side in range(2):
            gacc[g, side] = jnp.zeros((BLOCK, HDIM), F32)

    def load_block(shard, b):
        rows = slice(b * BLOCK, (b + 1) * BLOCK)
        query = jnp.concatenate([qb[shard, rows, j * HDIM : (j + 1) * HDIM] for j in range(4)], axis=0)
        grad = jnp.concatenate([gb[shard, rows, j * HDIM : (j + 1) * HDIM] for j in range(4)], axis=0)
        tile = stats[shard, :, rows]
        lse = jnp.concatenate([tile[j : j + 1] for j in range(4)], axis=1)
        delta = jnp.concatenate([tile[4 + j : 5 + j] for j in range(4)], axis=1)
        return query, grad, lse, delta

    def attend(pairs, lses, query, grad, delta):
        count = len(pairs)
        keys = jnp.concatenate([k for k, _ in pairs], axis=0)
        values = jnp.concatenate([v for _, v in pairs], axis=0)
        scores = lax.dot_general(keys, query, NT, preferred_element_type=F32) * (SCALE * LOG2E)
        scores = jnp.concatenate([scores[k * BLOCK : (k + 1) * BLOCK] - lses[k] for k in range(count)], axis=0)
        probs = jnp.exp2(scores)
        prob_grad = lax.dot_general(values, grad, NT, preferred_element_type=F32)
        score_grad = (probs * (prob_grad - delta)).astype(BF)
        value_entry = jnp.dot(probs.astype(BF), grad, preferred_element_type=F32)
        key_entry = jnp.dot(score_grad, query, preferred_element_type=F32)
        turned = lax.dot_general(keys, score_grad, TN, preferred_element_type=F32)
        cut = [slice(k * BLOCK, (k + 1) * BLOCK) for k in range(count)]
        return [key_entry[c] for c in cut], [value_entry[c] for c in cut], turned

    def window(k, add):
        shard = lax.rem(y - offset_of(k) + N, N)
        remote(hal.at[0, shard], hal.at[0, shard], hn_s.at[shard], hn_r.at[shard], shifted(di=1)).wait_recv()
        remote(hal.at[1, shard], hal.at[1, shard], hp_s.at[shard], hp_r.at[shard], shifted(di=1)).wait_recv()
        for b in range(2):
            query, grad, lse, delta = load_block(shard, b)
            width = ints[shard, 0, 6 + b]
            block_id = ((z * N + shard) * N + i) * 2 + b
            total = None
            for group in WINDOW_GROUPS:
                pairs, lses = [], []
                for e in group:
                    at = b + e - 2
                    if at < 0:
                        pairs.append((hal[0, shard, at + 2, 0], hal[0, shard, at + 2, 1]))
                    elif at >= 2:
                        pairs.append((hal[1, shard, at - 2, 0], hal[1, shard, at - 2, 1]))
                    else:
                        slot = z * 8 + shard * 2 + at
                        pairs.append((kvu[slot, 0], kvu[slot, 1]))
                    target = block_id + e - 2
                    ok = (abs(e - 2) <= width) & (target >= 0) & (target < 128)
                    lses.append(lse + jnp.where(ok, 0.0, 1e6).astype(F32))
                dks, dvs, turned = attend(pairs, lses, query, grad, delta)
                total = turned if total is None else total + turned
                for e, dk_e, dv_e in zip(group, dks, dvs):
                    at = b + e
                    if b == 0 or at == 5:
                        acc[shard, at, 0] = dk_e
                        acc[shard, at, 1] = dv_e
                    else:
                        acc[shard, at, 0] += dk_e
                        acc[shard, at, 1] += dv_e
            if add:
                dqt[2 * k + b] += total
            else:
                dqt[2 * k + b] = total
        for n, start in enumerate((0, 4)):
            for b in range(2):
                dhb[n, shard, b, 0] = (acc[shard, start + b, 0] * SCALE).astype(BF)
                dhb[n, shard, b, 1] = acc[shard, start + b, 1].astype(BF)
        to, spot = preceding(shard)
        remote(dhb.at[0, shard], hrn.at[spot], dn_s.at[shard], dn_r.at[spot], to).start()
        to, spot = following(shard)
        remote(dhb.at[1, shard], hrp.at[spot], dp_s.at[shard], dp_r.at[spot], to).start()

    def wait_queries(k):
        dy = offset_of(k)
        for side, (ref, dst) in enumerate(((q_ref, qb), (g_ref, gb))):
            n = 2 * (dy - 1) + side
            remote(
                ref.at[:, columns(y, 512)], dst.at[y], q_s.at[n], q_r.at[n], shifted(dy=1)
            ).wait_recv()

    for one in stay:
        one.wait()
    def early(k, carry):
        @pl.when(k > 0)
        def _():
            wait_queries(k)

        window(k, False)
        return carry

    lax.fori_loop(0, 1, early, 0)
    ask(2)
    pass_on(3)
    pass_on(2)
    lax.fori_loop(1, 3, early, 0)

    for dy in range(N):
        for dz in range(1, N):
            if dz == 2 or dz == (3 if dy in UPWARD else 1):
                ag_copies[dy, dz].wait_recv()
    for g in range(2):
        gsend[g] = kvu[block_slot(glob_ref[g])]
    gl_copies = [
        remote(gsend, grecv.at[di], gl_s.at[di - 1], gl_r.at[di - 1], shifted(di=di)) for di in range(1, N)
    ]
    for one in gl_copies:
        one.start()
    grecv[0] = gsend[...]

    def random(k, carry):
        @pl.when(k == 3)
        def _():
            wait_queries(k)

        shard = lax.rem(y - offset_of(k) + N, N)
        for b in range(2):
            query, grad, lse, delta = load_block(shard, b)
            total = None
            for group in RANDOM_GROUPS:
                slots = [ints[shard, 0, b * 3 + r] for r in group]
                pairs = [(kvu[s, 0], kvu[s, 1]) for s in slots]
                dks, dvs, turned = attend(pairs, [lse] * len(group), query, grad, delta)
                total = turned if total is None else total + turned
                for r, dk_e, dv_e in zip(group, dks, dvs):
                    ent[shard, 1 + b * 3 + r, 0] = (dk_e * SCALE).astype(BF)
                    ent[shard, 1 + b * 3 + r, 1] = dv_e.astype(BF)
            dqt[2 * k + b] += total
        return carry

    lax.fori_loop(0, N, random, 0)

    def named(slot):
        total = None
        for shard in range(N):
            one = ent[shard, ints[shard, 1, slot]].astype(F32)
            total = one if total is None else total + one
        return total

    rs_copies = {}

    def fill(dz, dy):
        shard = lax.rem(y + dy, N)
        to = lax.rem(z + dz, N)

        def put(b, carry):
            rsb[dz - 1, dy, b] = named(to * 8 + shard * 2 + b).astype(BF)
            return carry

        lax.fori_loop(0, 2, put, 0)

    def rs_send(dz, dy, dst, to):
        n = dy * 3 + dz - 1
        rs_copies[dz, dy] = remote(rsb.at[dz - 1, dy], dst, rs_s.at[n], rs_r.at[n], to)
        rs_copies[dz, dy].start()

    def rs_fill(dys):
        for dy in dys:
            for dz in range(1, N):
                fill(dz, dy)

    def rs_first(dys):
        for dy in dys:
            for dz in (2, 1, 3):
                rs_send(dz, dy, rsr.at[dz - 1, dy], shifted(dz=dz))

    rs_fill(CLOSING[:2])
    rs_first(CLOSING[:2])

    for one in gl_copies:
        one.wait_recv()
    globe = []
    for g in range(2):
        source = lax.rem(i - lax.rem(glob_ref[g] // 2, N) + N, N)
        globe.append(source)

    def dq_copy(k):
        dy = offset_of(k)
        shard = lax.rem(y - dy + N, N)
        return remote(
            dqb.at[shard], dq.at[:, columns(y, 512)], dq_s.at[dy - 1], dq_r.at[dy - 1], device(z, shard, i, h)
        )

    dq_home = pltpu.make_async_copy(dqb.at[y], dq.at[:, columns(y, 512)], loc.at[9])

    def whole(k, carry):
        shard = lax.rem(y - offset_of(k) + N, N)
        for b in range(2):
            query, grad, lse, delta = load_block(shard, b)
            pairs = [(grecv[globe[g], g, 0], grecv[globe[g], g, 1]) for g in range(2)]
            dks, dvs, turned = attend(pairs, [lse] * 2, query, grad, delta)
            for g in range(2):
                gacc[g, 0] += dks[g]
                gacc[g, 1] += dvs[g]
            dqt[2 * k + b] += turned
        return carry

    def give_query(k, carry):
        shard = lax.rem(y - offset_of(k) + N, N)
        for b in range(2):
            done = (jnp.transpose(dqt[2 * k + b]) * SCALE).astype(BF)
            for j in range(4):
                dqb[shard, b * BLOCK : (b + 1) * BLOCK, j * HDIM : (j + 1) * HDIM] = done[
                    j * BLOCK : (j + 1) * BLOCK
                ]

        @pl.when(k == 0)
        def _():
            dq_home.start()

        @pl.when(k > 0)
        def _():
            dq_copy(k).start()

        return carry

    def late(k, carry):
        window(k, True)
        return carry

    lax.fori_loop(0, N, whole, 0)
    for g in range(2):
        dglb[2 * g] = (gacc[g, 0] * SCALE).astype(BF)
        dglb[2 * g + 1] = gacc[g, 1].astype(BF)
    g1_copies = [
        remote(dglb.at[lax.rem(i + di, N)], g1r.at[di - 1], g1_s.at[di - 1], g1_r.at[di - 1], shifted(di=di))
        for di in range(1, N)
    ]
    for one in g1_copies:
        one.start()
    lax.fori_loop(0, 3, give_query, 0)
    rs_fill(CLOSING[2:])
    for one in g1_copies:
        one.wait_recv()
    partial = dglb[i].astype(F32)
    for n in range(3):
        partial = partial + g1r[n].astype(F32)
    g2s[0] = partial.astype(BF)
    g2_copies = [
        remote(g2s.at[0], g2r.at[dz - 1], g2_s.at[dz - 1], g2_r.at[dz - 1], shifted(dz=dz)) for dz in range(1, N)
    ]
    for one in g2_copies:
        one.start()
    rs_first(CLOSING[2:])
    lax.fori_loop(3, 4, late, 0)
    lax.fori_loop(3, 4, give_query, 0)
    for one in g2_copies:
        one.wait_recv()
    for n in range(3):
        partial = partial + g2r[n].astype(F32)
    g2s[1] = partial.astype(BF)
    g3r[i] = g2s[1]
    g3_copies = [
        remote(g2s.at[1], g3r.at[i], g3_s.at[di - 1], g3_r.at[di - 1], shifted(di=di)) for di in range(1, N)
    ]
    for one in g3_copies:
        one.start()
    for one in g3_copies:
        one.wait_recv()
    for shard in range(N):
        remote(dhb.at[0, shard], hrn.at[shard], dn_s.at[shard], dn_r.at[shard], shifted(di=1)).wait_recv()
        remote(dhb.at[1, shard], hrp.at[shard], dp_s.at[shard], dp_r.at[shard], shifted(di=1)).wait_recv()

    out_copies, home = [], []
    for dy in CLOSING:
        shard = lax.rem(y + dy, N)
        for dz in range(1, N):
            rs_copies[dz, dy].wait_recv()

        def close(b, carry, shard=shard, dy=dy):
            block_id = ((z * N + shard) * N + i) * 2 + b
            extra = named(z * 8 + shard * 2 + b)
            for side in range(2):
                total = acc[shard, 2 + b, side] * (SCALE if side == 0 else 1.0) + extra[side]
                total = total + hrn[shard, b, side].astype(F32) + hrp[shard, b, side].astype(F32)
                for n in range(3):
                    total = total + rsr[n, dy, b, side].astype(F32)
                for g in range(2):
                    hit = (jnp.zeros((BLOCK, HDIM), I32) + glob_ref[g]) == block_id
                    total = total + jnp.where(hit, g3r[2 * g + side].astype(F32), 0.0)
                outb[shard, b, side] = total.astype(BF)
            return carry

        lax.fori_loop(0, 2, close, 0)
        for dh in range(2):
            b = lax.rem(h + dh, 2)
            if (dy, dh) == (0, 0):
                home.append(pltpu.make_async_copy(outb.at[shard, b], dkv.at[h * N + y], loc.at[10]))
                home[-1].start()
            else:
                n = YH.index((dy, dh))
                out_copies.append(
                    remote(
                        outb.at[shard, b], dkv.at[h * N + y], out_s.at[n], out_r.at[n], shifted(dy=dy, dh=dh)
                    )
                )
                out_copies[-1].start()
    for one in out_copies + home + [dq_home]:
        one.wait()
    for k in range(1, N):
        dq_copy(k).wait()
    for one in list(kv_copies.values()) + list(q_copies.values()) + it_copies + st_copies:
        one.wait_send()
    for one in list(ag_copies.values()) + list(rs_copies.values()):
        one.wait_send()
    for one in hn_copies + hp_copies + gl_copies + g1_copies + g2_copies + g3_copies:
        one.wait_send()
    for shard in range(N):
        remote(dhb.at[0, shard], hrn.at[shard], dn_s.at[shard], dn_r.at[shard], shifted(di=1)).wait_send()
        remote(dhb.at[1, shard], hrp.at[shard], dp_s.at[shard], dp_r.at[shard], shifted(di=1)).wait_send()


def hand_over(dq, dkv, dq_out, dk_out, dv_out, wide, tall, sems_in, sems_out):
    come = [pltpu.make_async_copy(dq.at[pl.ds(64 * n, 64)], wide.at[n], sems_in.at[n]) for n in range(4)]
    leave = [pltpu.make_async_copy(wide.at[n], dq_out.at[pl.ds(64 * n, 64)], sems_out.at[n]) for n in range(4)]
    whole_in = pltpu.make_async_copy(dkv, tall, sems_in.at[4])
    for one in come:
        one.start()
    whole_in.start()
    for first, then in zip(come, leave):
        first.wait()
        then.start()
    whole_in.wait()
    for n in range(8):
        for side, ref in enumerate((dk_out, dv_out)):
            leave.append(
                pltpu.make_async_copy(
                    tall.at[n, side], ref.at[:, n * HDIM : (n + 1) * HDIM], sems_out.at[4 + 2 * n + side]
                )
            )
            leave[-1].start()
    for one in leave:
        one.wait()


HBM = pl.BlockSpec(memory_space=pltpu.HBM)
SMEM = pl.BlockSpec(memory_space=pltpu.SMEM)
DMA = pltpu.SemaphoreType.DMA


def on_device(
    queries, key_heads, value_heads, output, output_grad, log_totals, random_blocks, window_width, global_blocks
):
    shape = jax.ShapeDtypeStruct
    tile = (BLOCK, HDIM)
    twice = lambda n: [DMA((n,)), DMA((n,))]
    results = pl.pallas_call(
        fused,
        out_shape=(
            shape((256, 2048), BF),
            shape((8, 2) + tile, BF),
        ),
        in_specs=[SMEM, SMEM, SMEM] + [HBM] * 6,
        out_specs=(HBM, HBM),
        scratch_shapes=[
            pltpu.VMEM((2, 256, 2048), BF),
            pltpu.VMEM((16, 256), F32),
            pltpu.VMEM((N, 8, 256), F32),
            pltpu.VMEM((8, 2) + tile, BF),
            pltpu.VMEM((8, 128), I32),
            pltpu.VMEM((N, 8, 128), I32),
            pltpu.SMEM((N, 8, 128), I32),
            pltpu.VMEM((N, 8, 256), F32),
            pltpu.VMEM((N, 256, 512), BF),
            pltpu.VMEM((N, 256, 512), BF),
            pltpu.VMEM((32, 2) + tile, BF),
            pltpu.VMEM((2, N, 2, 2) + tile, BF),
            pltpu.VMEM((2, 2) + tile, BF),
            pltpu.VMEM((N, 2, 2) + tile, BF),
            pltpu.VMEM((8, HDIM, 512), F32),
            pltpu.VMEM((N, 6, 2) + tile, F32),
            pltpu.VMEM((2, N, 2, 2) + tile, BF),
            pltpu.VMEM((N, 2, 2) + tile, BF),
            pltpu.VMEM((N, 2, 2) + tile, BF),
            pltpu.VMEM((N, 7, 2) + tile, BF),
            pltpu.VMEM((3, N, 2, 2) + tile, BF),
            pltpu.VMEM((3, N, 2, 2) + tile, BF),
            pltpu.VMEM((2, 2) + tile, F32),
            pltpu.VMEM((4,) + tile, BF),
            pltpu.VMEM((3,) + tile, BF),
            pltpu.VMEM((2,) + tile, BF),
            pltpu.VMEM((3,) + tile, BF),
            pltpu.VMEM((4,) + tile, BF),
            pltpu.VMEM((N, 256, 512), BF),
            pltpu.VMEM((N, 2, 2) + tile, BF),
            DMA((12,)),
            DMA((16,)),
        ]
        + twice(7) + twice(6) + twice(3) + twice(3) + twice(12) + twice(4) + twice(4) + twice(3)
        + twice(4) + twice(4) + twice(12) + twice(3) + twice(3) + twice(3) + twice(3) + twice(7),
        compiler_params=pltpu.CompilerParams(
            collective_id=0, has_side_effects=True, vmem_limit_bytes=60 * 2**20
        ),
        name="fused",
    )(
        global_blocks, random_blocks, window_width, queries, key_heads, value_heads, output, output_grad, log_totals
    )
    return pl.pallas_call(
        hand_over,
        out_shape=(shape((256, 2048), BF), shape((BLOCK, 1024), BF), shape((BLOCK, 1024), BF)),
        in_specs=[HBM] * 2,
        out_specs=(HBM, HBM, HBM),
        scratch_shapes=[
            pltpu.VMEM((4, 64, 2048), BF),
            pltpu.VMEM((8, 2) + tile, BF),
            DMA((5,)),
            DMA((20,)),
        ],
        compiler_params=pltpu.CompilerParams(vmem_limit_bytes=60 * 2**20),
        name="hand_over",
    )(*results)


def solution(mesh):
    placed = (
        P(("outer", "inner"), "head"),
        P(("outer", "inner", "head"), None),
        P(("outer", "inner", "head"), None),
        P(("outer", "inner"), "head"),
        P(("outer", "inner"), "head"),
        P("head", ("outer", "inner")),
        P(("outer", "inner"), None),
        P(("outer", "inner")),
        P(),
    )
    return jax.shard_map(
        on_device,
        mesh=mesh,
        in_specs=placed,
        out_specs=(
            P(("outer", "inner"), "head"),
            P(("outer", "inner", "head"), None),
            P(("outer", "inner", "head"), None),
        ),
        check_vma=False,
    )
```
